128 devices in a mesh: set: 4 (over x), cand: 32 (over z, y, core).
Axes of the slice: x: 4, y: 4, z: 4, core: 2. Of those that a mesh axis runs over, the one named last changes fastest.
Arguments:
- panel_rows: bfloat16 [4, 65536, 512], P('set', 'cand'), may hold values from -10 to 10
- sketch: bfloat16 [4, 512, 32], P('set'), may hold values from -0.25 to 0.25
- accumulator: float32 [4, 256, 256, 256], P('set', 'cand'), may hold values from -6 to 6
- left_block: int32 [4, 32, 128, 2], P('set', 'cand'), may hold values from 0 to 7
- right_block: int32 [4, 32, 128, 2], P('set', 'cand'), may hold values from 0 to 255
- target_slot: int32 [4, 32, 128, 2], P('set', 'cand'), may hold values from 0 to 7
- slot_valid: int32 [4, 32, 128, 2], P('set', 'cand'), may hold values from 0 to 1, as said below
Outputs:
- updated: float32 [4, 256, 256, 256], P('set', 'cand')
The draws below stay inside these ranges and needn't reach their ends.
Inputs may be any that keep to these rules, and one draw needn't show every extreme that they name: `slot_valid`: padding slots still name blocks; some destination devices receive far more pairs than others.
All inputs are finite; a program needn't handle non-finite values. Where the reference program divides by a largest or mean magnitude, that divisor is 1e-20 or more.
Results may differ from the reference program's by a relative error of at most 0.02.
Values may be sent and summed in bfloat16 or wider, within the bound.
No kernel may reach another device: no remote copies, remote signals or barrier semaphores. Data moves between devices by JAX's collectives and lax.ppermute only.
A program may use at most 128 MiB of HBM per device.

```python
import jax
import jax.numpy as jnp
from jax import lax

W = 512
RANK = 32
BLOCK = 256
NB_DEV = 8
NT_DEV = 8
CAP = 2
NBS = 256
TARGETS = 256
N_SET = 4
N_CAND = 32
DEVICES = 128


def draw_panel_rows(key, part):
    key = jax.random.fold_in(key, 5)
    row_count = N_CAND * NB_DEV * BLOCK
    owner_device = jnp.arange(row_count) // (NB_DEV * BLOCK)
    column_group = jnp.arange(W) // (W // N_CAND)
    own_columns = (owner_device[:, None] == column_group[None, :]).astype(jnp.float32)
    rising = jnp.sqrt(1.0 + 2.0 * owner_device.astype(jnp.float32) / max(N_CAND - 1, 1))
    values = jax.random.normal(key, (N_SET, row_count, W), jnp.float32)
    shaped = 0.2 * values * (1.0 + 3.0 * own_columns)[None] * rising[None, :, None]
    return shaped.astype(jnp.bfloat16)


def draw_slot_valid(key, part):
    key = jax.random.fold_in(key, 9)
    device_count = N_SET * N_CAND
    hotness = jax.random.randint(jax.random.fold_in(key, 1), (device_count,), 0, 4)
    rolls = jax.random.randint(jax.random.fold_in(key, 2), (N_SET, N_CAND, device_count, CAP), 0, 16)
    limit = jnp.left_shift(2, hotness) - 1
    return (rolls < limit[None, None, :, None]).astype(jnp.int32)


def touch_ends(drawn, key, smallest, largest):
    longest = drawn.shape.index(max(drawn.shape))
    spots = []
    for shift in (0, 1):
        where = [jax.random.randint(jax.random.fold_in(key, axis), (), 0, length) for axis, length in enumerate(drawn.shape)]
        where[longest] = (where[longest] + shift) % drawn.shape[longest]
        spots.append(tuple(where))
    return drawn.at[spots[0]].set(smallest).at[spots[1]].set(largest)


def shard_levels(key, extent, cuts, smallest, high):
    gain = 1.0
    for axis_at, shards_of in cuts:
        steps = jax.random.uniform(jax.random.fold_in(jax.random.fold_in(key, 6), axis_at), (shards_of,), jnp.float32, smallest / len(cuts), high / len(cuts))
        gain = gain * jnp.repeat(jnp.exp(steps), extent[axis_at] // shards_of).reshape((-1,) + (1,) * (len(extent) - 1 - axis_at))
    return gain


def noise(own_key, shape, scale, most, cuts=(), kind=jnp.bfloat16):
    factor_of = shard_levels(own_key, shape, cuts, -0.22, 0.18) if cuts else 1.0
    drawn = jax.random.normal(own_key, shape, jnp.float32) * scale * factor_of
    return jnp.minimum(jnp.maximum(drawn, -most), most).astype(kind)


def setup_inputs(seed: int = 0) -> dict:
    key_list = jax.random.split(jax.random.key(seed), 8)
    return {
        "panel_rows": draw_panel_rows(jax.random.fold_in(key_list[7], 71), 0),
        "sketch": noise(key_list[1], (N_SET, W, RANK), W ** -0.5, 0.25, ((0, 4),)),
        "accumulator": noise(key_list[2], (N_SET, TARGETS, BLOCK, BLOCK), 1.0, 6.0, ((0, 4), (1, 32)), jnp.float32),
        "left_block": touch_ends(jax.random.randint(key_list[3], (N_SET, N_CAND, DEVICES, CAP), 0, NB_DEV), jax.random.fold_in(key_list[3], 1), 0, NB_DEV - 1).astype(jnp.int32),
        "right_block": touch_ends(jax.random.randint(key_list[4], (N_SET, N_CAND, DEVICES, CAP), 0, NBS), jax.random.fold_in(key_list[4], 1), 0, NBS - 1).astype(jnp.int32),
        "target_slot": touch_ends(jax.random.randint(key_list[5], (N_SET, N_CAND, DEVICES, CAP), 0, NT_DEV), jax.random.fold_in(key_list[5], 1), 0, NT_DEV - 1).astype(jnp.int32),
        "slot_valid": draw_slot_valid(jax.random.fold_in(key_list[7], 71), 0),
    }


def compress_set(panel_set, sketch_set):
    sketched = jnp.dot(panel_set.astype(jnp.float32), sketch_set.astype(jnp.float32), preferred_element_type=jnp.float32).astype(jnp.bfloat16)
    summed_sketch = lax.dot_general(panel_set.astype(jnp.float32), sketched.astype(jnp.float32), (((0,), (0,)), ((), ())), preferred_element_type=jnp.float32)
    gram_matrix = jnp.dot(summed_sketch.T, summed_sketch, precision=lax.Precision.HIGHEST)
    lower_factor = jnp.linalg.cholesky(gram_matrix)
    basis_rows = jax.scipy.linalg.solve_triangular(lower_factor, summed_sketch.T, lower=True).astype(jnp.bfloat16)
    blocks = panel_set.reshape(NBS, BLOCK, W)
    projected = jnp.einsum('rw,nbw->nrb', basis_rows.astype(jnp.float32), blocks.astype(jnp.float32))
    block_scale = (jnp.max(jnp.abs(projected), axis=(1, 2)) + 1e-06).astype(jnp.bfloat16)
    factor = (projected / block_scale.astype(jnp.float32)[:, None, None]).astype(jnp.bfloat16)
    return (factor, block_scale)

def reference(panel_rows, sketch, accumulator, left_block, right_block, target_slot, slot_valid):
    factor_list = []
    scale_list = []
    for set_index in range(N_SET):
        factor, block_scale = compress_set(panel_rows[set_index], sketch[set_index])
        factor_list.append(factor)
        scale_list.append(block_scale)
    all_factor = jnp.stack(factor_list)
    all_scale = jnp.stack(scale_list)
    set_ids = jnp.arange(N_SET, dtype=jnp.int32)[:, None, None]
    cand_ids = jnp.arange(N_CAND, dtype=jnp.int32)[None, :, None]
    initial = accumulator.reshape(DEVICES, NT_DEV, BLOCK, BLOCK)
    slot_count = DEVICES * CAP

    def per_device(device_index):
        left_index = cand_ids * NB_DEV + jnp.take(left_block, device_index, axis=2).astype(jnp.int32)
        right_index = jnp.take(right_block, device_index, axis=2).astype(jnp.int32)
        target_index = jnp.take(target_slot, device_index, axis=2)
        valid_here = jnp.take(slot_valid, device_index, axis=2)
        left_pairs = all_factor[set_ids, left_index]
        right_pairs = all_factor[set_ids, right_index]
        pair_weight = (valid_here.astype(jnp.float32) * all_scale[set_ids, left_index].astype(jnp.float32) * all_scale[set_ids, right_index].astype(jnp.float32)).astype(jnp.bfloat16)
        scaled_left = (pair_weight.astype(jnp.float32)[..., None, None] * left_pairs.astype(jnp.float32)).astype(jnp.bfloat16)
        scaled_left = scaled_left.reshape(slot_count, RANK, BLOCK)
        right_pairs = right_pairs.reshape(slot_count, RANK, BLOCK)
        dense_terms = jnp.einsum('prb,pre->pbe', scaled_left.astype(jnp.float32), right_pairs.astype(jnp.float32))
        one_hot = (target_index.reshape(slot_count)[:, None] == jnp.arange(NT_DEV, dtype=jnp.int32)[None, :]).astype(jnp.float32)
        summed = jnp.einsum('pt,pbe->tbe', one_hot, dense_terms)
        return jnp.take(initial, device_index, axis=0) - summed
    updated = lax.map(per_device, jnp.arange(DEVICES, dtype=jnp.int32))
    return updated.reshape(N_SET, TARGETS, BLOCK, BLOCK)
```

```python
import jax
import jax.numpy as jnp
from jax import lax
from jax.experimental import pallas as pl
from jax.experimental.pallas import tpu as pltpu
from jax.sharding import PartitionSpec as P

W = 512
RANK = 32
BLOCK = 256
NB_DEV = 8
NT_DEV = 8
N_SET = 4
N_CAND = 32
HALF = RANK // 2
ROWS = NB_DEV * BLOCK
A_ROWS = 4 * RANK + 16
B_ROWS = 4 * RANK
MSG = A_ROWS + B_ROWS
SLOTS = 2
PER_CHUNK = 8
LIST = 128
ZERO = NB_DEV * N_CAND
f32, bf16, i32 = jnp.float32, jnp.bfloat16, jnp.int32
VMEM = pl.BlockSpec(memory_space=pltpu.VMEM)
SMEM = pl.BlockSpec(memory_space=pltpu.SMEM)
ANY = pl.BlockSpec(memory_space=pl.ANY)
NT = (((1,), (1,)), ((), ()))
TN = (((0,), (0,)), ((), ()))


def params(mib=40):
    return pltpu.CompilerParams(vmem_limit_bytes=mib * 1024 * 1024)


def from_cand(x, dz, dy, dcore=0):
    pairs = []
    for me in range(N_CAND):
        z, y, core = me // 8, (me // 2) % 4, me % 2
        source = ((z + dz) % 4) * 8 + ((y + dy) % 4) * 2 + (core ^ dcore)
        pairs.append((source, me))
    return lax.ppermute(x, "cand", pairs)


def from_set(x, d):
    return lax.ppermute(x, "set", [((me + d) % N_SET, me) for me in range(N_SET)])


def sketch_kernel(place, rows, sketch, keep, give, total):
    step = pl.program_id(0)

    @pl.when(step == 0)
    def _():
        total[...] = jnp.zeros_like(total)

    sketched = jnp.dot(rows[...], sketch[...], preferred_element_type=f32).astype(bf16)
    total[...] += lax.dot_general(sketched, rows[...], TN, preferred_element_type=f32)

    @pl.when(step == pl.num_programs(0) - 1)
    def _():
        core = place[1] % 2
        keep[...] = total[pl.ds(pl.multiple_of(core * HALF, HALF), HALF), :]
        give[...] = total[pl.ds(pl.multiple_of((1 - core) * HALF, HALF), HALF), :]


def sketch_call(place, rows, sketch):
    step = 512
    half = jax.ShapeDtypeStruct((HALF, W), f32)
    return pl.pallas_call(
        sketch_kernel,
        grid=(ROWS // step,),
        out_shape=(half, half),
        in_specs=[
            SMEM,
            pl.BlockSpec((step, W), lambda i: (i, 0)),
            pl.BlockSpec((W, RANK), lambda i: (0, 0)),
        ],
        out_specs=(pl.BlockSpec((HALF, W), lambda i: (0, 0)),) * 2,
        scratch_shapes=[pltpu.VMEM((RANK, W), f32)],
        compiler_params=params(),
        name="sketch",
    )(place, rows, sketch)


def sum_core_kernel(keep, got, slots, out):
    out[0:HALF, :] = keep[...] + got[...]
    out[HALF:, :] = jnp.zeros((8, W), f32)
    out[HALF:, 0:128] = slots[...]


def sum_y_kernel(r0, r1, r2, r3, out):
    out[0:HALF, :] = (r0[0:HALF, :] + r2[0:HALF, :]) + (r1[0:HALF, :] + r3[0:HALF, :])
    for k, r in enumerate((r0, r1, r2, r3)):
        out[HALF:, k * 128 : (k + 1) * 128] = r[HALF:, 0:128]


def sum_z_kernel(r0, r1, r2, r3, out):
    out[0:HALF, :] = (r0[0:HALF, :] + r2[0:HALF, :]) + (r1[0:HALF, :] + r3[0:HALF, :])
    for k, r in enumerate((r0, r1, r2, r3)):
        out[HALF + 8 * k : HALF + 8 * (k + 1), :] = r[HALF:, :]


def small_call(kernel, rows, name, *args):
    return pl.pallas_call(
        kernel,
        out_shape=jax.ShapeDtypeStruct((rows, W), f32),
        in_specs=[VMEM] * len(args),
        out_specs=VMEM,
        compiler_params=params(),
        name=name,
    )(*args)


def factor_kernel(place, own, other, rows_hbm, out_a, out_b, rows, sem):
    copy = pltpu.make_async_copy(rows_hbm, rows, sem)
    copy.start()
    first = place[1] % 2 == 0
    mine, theirs = own[0:HALF, :], other[0:HALF, :]
    summed = jnp.concatenate(
        [jnp.where(first, mine, theirs), jnp.where(first, theirs, mine)], axis=0
    )
    padded = jnp.concatenate([summed, jnp.zeros((96, W), f32)], axis=0)
    gram = lax.dot_general(
        summed, padded, NT, precision=lax.Precision.HIGHEST, preferred_element_type=f32
    )
    lane = lax.broadcasted_iota(i32, (RANK, 128), 1)
    line = lax.broadcasted_iota(i32, (RANK, 128), 0)
    work = gram + jnp.where(lane == line + RANK, 1.0, 0.0)
    for k in range(RANK - 1):
        column = jnp.broadcast_to(work[:, k : k + 1], (RANK, 128))
        pivot_row = work[k : k + 1, :] / column[k : k + 1, :]
        work = work - jnp.where(line > k, column, 0.0) * pivot_row
    pivots = jnp.sum(jnp.where(lane == line, work, 0.0), axis=1, keepdims=True)
    inverse = work * lax.rsqrt(pivots)
    shifted = jnp.concatenate([jnp.zeros((32, W), f32), summed, jnp.zeros((64, W), f32)], axis=0)
    basis = jnp.dot(
        inverse, shifted, precision=lax.Precision.HIGHEST, preferred_element_type=f32
    ).astype(bf16)
    copy.wait()
    index = lax.broadcasted_iota(i32, (16, BLOCK), 0)
    scales = jnp.zeros((16, BLOCK), f32)
    for b in range(NB_DEV):
        projected = lax.dot_general(
            basis, rows[b * BLOCK : (b + 1) * BLOCK, :], NT, preferred_element_type=f32
        )
        most = jnp.max(jnp.max(jnp.abs(projected), axis=0, keepdims=True), axis=1, keepdims=True)
        scale = (most + 1e-06).astype(bf16).astype(f32)
        factor = (projected / scale).astype(bf16)
        scales = jnp.where(index == b, scale, scales)
        if b < 4:
            out_a[b * RANK : (b + 1) * RANK, :] = factor
        else:
            out_b[(b - 4) * RANK : (b - 3) * RANK, :] = factor
    out_a[4 * RANK :, :] = scales.astype(bf16)


def factor_call(place, own, other, rows):
    return pl.pallas_call(
        factor_kernel,
        out_shape=(
            jax.ShapeDtypeStruct((A_ROWS, BLOCK), bf16),
            jax.ShapeDtypeStruct((B_ROWS, BLOCK), bf16),
        ),
        in_specs=[SMEM, VMEM, VMEM, ANY],
        out_specs=(VMEM, VMEM),
        scratch_shapes=[pltpu.VMEM((ROWS, W), bf16), pltpu.SemaphoreType.DMA],
        compiler_params=params(),
        name="factor",
    )(place, own, other, rows)


def plan_kernel(place, own, other, *refs):
    lists, (gathered, picked_v, picked, at, sem) = refs[:N_SET], refs[N_SET:]
    me_set, me = place[0], place[1]
    me_z, me_y, me_core = me // 8, (me // 2) % 4, me % 2
    for core, r in enumerate((own, other)):
        for z in range(4):
            for y in range(4):
                s = (core * 4 + z) * 4 + y
                gathered[s * 8 : (s + 1) * 8, :] = r[
                    HALF + 8 * z : HALF + 8 * (z + 1), y * 128 : (y + 1) * 128
                ].astype(bf16)
    line = lax.broadcasted_iota(i32, (16, 128), 0)
    lane = lax.broadcasted_iota(i32, (16, 128), 1)
    wanted = ((me_set + line) % N_SET) * N_CAND + me
    hot = jnp.where((lane == wanted) & (line < N_SET), 1.0, 0.0).astype(bf16)
    values = lax.dot_general(hot, gathered[...], NT, preferred_element_type=f32)
    picked_v[...] = values[0:8, :].astype(i32)
    copy = pltpu.make_async_copy(picked_v, picked, sem)
    copy.start()
    copy.wait()
    for gr in range(N_SET):
        out = lists[gr]
        for t in range(NT_DEV):
            at[t] = 0

        def count(s, carry):
            for slot in range(SLOTS):
                t = picked[gr, s * 8 + 4 + slot]
                at[t] = at[t] + picked[gr, s * 8 + 6 + slot]
            return carry

        lax.fori_loop(0, N_CAND, count, 0)
        start = 0
        for t in range(NT_DEV):
            chunks = (at[t] + (PER_CHUNK - 1)) // PER_CHUNK
            out[2 * LIST + t] = chunks
            at[t] = start
            start = start + chunks * PER_CHUNK

        def put(s, carry):
            s_core, s_z, s_y = s // 16, (s // 4) % 4, s % 4
            if gr == 2:
                sender = ((s_z + me_z) % 4) * 8 + ((s_y + me_y) % 4) * 2 + (s_core + me_core) % 2
            else:
                sender = s
            for slot in range(SLOTS):
                left = sender * NB_DEV + picked[gr, s * 8 + slot]
                right = picked[gr, s * 8 + 2 + slot]
                if gr != 2:
                    owner = right // NB_DEV
                    r_z, r_y, r_core = owner // 8, (owner // 2) % 4, owner % 2
                    owner = (
                        ((r_core + me_core) % 2) * 4 + (r_z - me_z + 4) % 4
                    ) * 4 + (r_y - me_y + 4) % 4
                    right = owner * NB_DEV + right % NB_DEV
                t = picked[gr, s * 8 + 4 + slot]
                valid = picked[gr, s * 8 + 6 + slot]

                @pl.when(valid != 0)
                def _():
                    spot = at[t]
                    out[spot] = left
                    out[LIST + spot] = right
                    at[t] = spot + 1

            return carry

        lax.fori_loop(0, N_CAND, put, 0)
        end = 0
        for t in range(NT_DEV):
            end = end + out[2 * LIST + t] * PER_CHUNK

            def fill(spot, carry):
                out[spot] = ZERO
                out[LIST + spot] = 0
                return carry

            lax.fori_loop(at[t], end, fill, 0)


def plan_call(place, own, other):
    return pl.pallas_call(
        plan_kernel,
        out_shape=(jax.ShapeDtypeStruct((1024,), i32),) * N_SET,
        in_specs=[SMEM, VMEM, VMEM],
        out_specs=(SMEM,) * N_SET,
        scratch_shapes=[
            pltpu.VMEM((N_CAND * 8, 128), bf16),
            pltpu.VMEM((8, N_CAND * 8), i32),
            pltpu.SMEM((8, N_CAND * 8), i32),
            pltpu.SMEM((NT_DEV,), i32),
            pltpu.SemaphoreType.DMA,
        ],
        compiler_params=params(),
        name="plan",
    )(place, own, other)


def spread(factors, scales):
    for p in range(N_CAND):
        scales[p * NB_DEV : (p + 1) * NB_DEV, :] = factors[
            p, 4 * RANK : 4 * RANK + 16, 0:128
        ].astype(f32)[0:NB_DEV, :]
    scales[ZERO : ZERO + 8, :] = jnp.zeros((8, 128), f32)


def block_at(factors, b):
    p, j = (b & (ZERO - 1)) // NB_DEV, b % NB_DEV
    off = pl.multiple_of(j * RANK + jnp.where(j >= 4, 16, 0), 16)
    return factors.at[p, pl.ds(off, RANK), :]


def expand(pairs, t, factors, scales, lefts, rights, start, total):
    def chunk(q, carry):
        for k in range(PER_CHUNK):
            spot = start + q * PER_CHUNK + k
            left, right = pairs[spot], pairs[LIST + spot]
            weight = scales[pl.ds(left, 1), :] * scales[pl.ds(right, 1), :]
            weight = weight.astype(bf16).astype(f32)
            weight = jnp.concatenate([weight, weight], axis=1)
            here = slice(k * RANK, (k + 1) * RANK)
            lefts[here, :] = (block_at(factors, left)[...].astype(f32) * weight).astype(bf16)
            rights[here, :] = block_at(factors, right)[...]
        total[...] += lax.dot_general(lefts[...], rights[...], TN, preferred_element_type=f32)
        return carry

    total[...] = jnp.zeros_like(total)
    chunks = pairs[2 * LIST + t]
    lax.fori_loop(0, chunks, chunk, 0)
    return start + chunks * PER_CHUNK


WORK = [
    pltpu.VMEM((N_CAND, MSG, BLOCK), bf16),
    pltpu.VMEM((ZERO + 8, 128), f32),
    pltpu.VMEM((RANK * PER_CHUNK, BLOCK), bf16),
    pltpu.VMEM((RANK * PER_CHUNK, BLOCK), bf16),
    pltpu.VMEM((BLOCK, BLOCK), f32),
]


def collect(pieces, factors, sems):
    copies = []
    for core in range(2):
        for k in range(4):
            a, b = pieces[core * 8 + k], pieces[core * 8 + 4 + k]
            copies.append(
                (a, factors.at[pl.ds(core * 16 + k * 4, 4), pl.ds(0, A_ROWS), :])
            )
            for z in range(4):
                copies.append(
                    (b.at[z], factors.at[core * 16 + z * 4 + k, pl.ds(A_ROWS, B_ROWS), :])
                )
    started = []
    for n, (source, target) in enumerate(copies):
        copy = pltpu.make_async_copy(source, target, sems.at[n])
        copy.start()
        started.append(copy)
    for copy in started:
        copy.wait()


def send_kernel(next_list, last_list, *refs):
    pieces, (to_next, to_last), work = refs[:16], refs[16:18], refs[18:]
    factors, scales, lefts, rights, total, sems = work
    collect(pieces, factors, sems)
    spread(factors, scales)
    start = [0, 0]
    for t in range(NT_DEV):
        for n, (pairs, out) in enumerate(((next_list, to_next), (last_list, to_last))):
            start[n] = expand(pairs, t, factors, scales, lefts, rights, start[n], total)
            out[t] = total[...].astype(bf16)


def send_call(next_list, last_list, pieces):
    out = jax.ShapeDtypeStruct((NT_DEV, BLOCK, BLOCK), bf16)
    return pl.pallas_call(
        send_kernel,
        out_shape=(out, out),
        in_specs=[SMEM, SMEM] + [ANY] * 16,
        out_specs=(VMEM, VMEM),
        scratch_shapes=WORK + [pltpu.SemaphoreType.DMA((40,))],
        compiler_params=params(),
        name="send_pairs",
    )(next_list, last_list, *pieces)


def own_kernel(own_list, base, *refs):
    pieces, out, work = refs[:16], refs[16], refs[17:]
    factors, scales, lefts, rights, total, sems = work
    collect(pieces, factors, sems)
    spread(factors, scales)
    start = 0
    for t in range(NT_DEV):
        start = expand(own_list, t, factors, scales, lefts, rights, start, total)
        out[t] = base[t] - total[...]


def own_call(own_list, base, pieces):
    return pl.pallas_call(
        own_kernel,
        out_shape=jax.ShapeDtypeStruct((NT_DEV, BLOCK, BLOCK), f32),
        in_specs=[SMEM, VMEM] + [ANY] * 16,
        out_specs=VMEM,
        scratch_shapes=WORK + [pltpu.SemaphoreType.DMA((40,))],
        compiler_params=params(),
        name="own_pairs",
    )(own_list, base, *pieces)


def far_kernel(far_list, base, gathered, out, factors, scales, lefts, rights, total, sem):
    copy = pltpu.make_async_copy(gathered, factors, sem)
    copy.start()
    copy.wait()
    spread(factors, scales)
    start = 0
    for t in range(NT_DEV):
        start = expand(far_list, t, factors, scales, lefts, rights, start, total)
        out[t] = base[t] - total[...]


def far_call(far_list, base, gathered):
    return pl.pallas_call(
        far_kernel,
        out_shape=jax.ShapeDtypeStruct((NT_DEV, BLOCK, BLOCK), f32),
        in_specs=[SMEM, VMEM, ANY],
        out_specs=VMEM,
        scratch_shapes=WORK + [pltpu.SemaphoreType.DMA],
        compiler_params=params(),
        name="far_pairs",
    )(far_list, base, gathered)


def per_device(panel_rows, sketch, accumulator, left_block, right_block, target_slot, slot_valid):
    rows = panel_rows[0]
    place = jnp.stack([lax.axis_index("set"), lax.axis_index("cand")]).astype(i32)

    keep, give = sketch_call(place, rows, sketch[0])
    got = from_cand(give, 0, 0, 1)
    slots = jnp.concatenate(
        [x[0, 0].T for x in (left_block, right_block, target_slot, slot_valid)], axis=0
    ).astype(f32)
    part = small_call(sum_core_kernel, HALF + 8, "sum_core", keep, got, slots)
    part = small_call(
        sum_y_kernel, HALF + 8, "sum_y", part, *[from_cand(part, 0, k) for k in (1, 2, 3)]
    )
    own = small_call(
        sum_z_kernel, HALF + 32, "sum_z", part, *[from_cand(part, k, 0) for k in (1, 2, 3)]
    )
    other = from_cand(own, 0, 0, 1)

    part_a, part_b = factor_call(place, own, other, rows)
    far = from_set(jnp.concatenate([part_a, part_b], axis=0), 2)
    all_a = jnp.stack([part_a] + [from_cand(part_a, 0, k) for k in (1, 2, 3)])
    all_b = jnp.stack([part_b] + [from_cand(part_b, k, 0) for k in (1, 2, 3)])
    here = [all_a] + [from_cand(all_a, k, 0) for k in (1, 2, 3)]
    here += [all_b] + [from_cand(all_b, 0, k) for k in (1, 2, 3)]
    pieces = here + [from_cand(x, 0, 0, 1) for x in here]

    own_list, next_list, far_list, last_list = plan_call(place, own, other)
    far_list = from_set(far_list, 2)
    far_all = lax.all_gather(far, "cand", axis=0, tiled=True).reshape(N_CAND, MSG, BLOCK)

    to_next, to_last = send_call(next_list, last_list, pieces)
    from_last = from_set(to_next, 3)
    from_next = from_set(to_last, 1)
    base = own_call(own_list, accumulator[0], pieces)
    base = far_call(far_list, base, far_all)
    return (base - (from_last.astype(f32) + from_next.astype(f32)))[None]


def solution(mesh):
    placed = (
        P("set", "cand", None),
        P("set", None, None),
        P("set", "cand", None, None),
        P("set", "cand", None, None),
        P("set", "cand", None, None),
        P("set", "cand", None, None),
        P("set", "cand", None, None),
    )
    return jax.shard_map(
        per_device,
        mesh=mesh,
        in_specs=placed,
        out_specs=P("set", "cand", None, None),
        check_vma=False,
    )
```

```python
import jax
import jax.numpy as jnp
from jax import lax
from jax.experimental import pallas as pl
from jax.experimental.pallas import tpu as pltpu
from jax.sharding import PartitionSpec as P

W = 512
RANK = 32
BLOCK = 256
NB_DEV = 8
NT_DEV = 8
N_SET = 4
N_CAND = 32
HALF = RANK // 2
ROWS = NB_DEV * BLOCK
MSG = NB_DEV * RANK + 16
SLOTS = 2
PER_CHUNK = 8
ENTRIES = N_CAND * SLOTS
ZERO = NB_DEV * N_CAND
LAST_US = 10
f32, bf16, i32 = jnp.float32, jnp.bfloat16, jnp.int32
VMEM = pl.BlockSpec(memory_space=pltpu.VMEM)
SMEM = pl.BlockSpec(memory_space=pltpu.SMEM)
ANY = pl.BlockSpec(memory_space=pl.ANY)
NT = (((1,), (1,)), ((), ()))
TN = (((0,), (0,)), ((), ()))


def params(mib=40):
    return pltpu.CompilerParams(vmem_limit_bytes=mib * 1024 * 1024)


def from_cand(x, leg, k, far=False):
    pairs = []
    for me in range(N_CAND):
        z, y, core = me // 8, (me // 2) % 4, me % 2
        if leg == core:
            y = (y + k) % 4
        else:
            z = (z + k) % 4
        pairs.append((z * 8 + y * 2 + core, me))
    if not far:
        return lax.ppermute(x, "cand", pairs)
    pairs = [
        ((me_set + 2) % N_SET * N_CAND + source, me_set * N_CAND + me)
        for me_set in range(N_SET)
        for source, me in pairs
    ]
    return lax.ppermute(x, ("set", "cand"), pairs)


def from_core(x):
    return lax.ppermute(x, "cand", [(me ^ 1, me) for me in range(N_CAND)])


def from_set(x, d):
    return lax.ppermute(x, "set", [((me + d) % N_SET, me) for me in range(N_SET)])


def sketch_kernel(place, rows, sketch, keep, give, total):
    step = pl.program_id(0)

    @pl.when(step == 0)
    def _():
        total[...] = jnp.zeros_like(total)

    sketched = lax.dot_general(sketch[...], rows[...], NT, preferred_element_type=f32)
    total[...] += jnp.dot(sketched.astype(bf16), rows[...], preferred_element_type=f32)

    @pl.when(step == pl.num_programs(0) - 1)
    def _():
        core = place[1] % 2
        keep[...] = total[pl.ds(pl.multiple_of(core * HALF, HALF), HALF), :]
        give[...] = total[pl.ds(pl.multiple_of((1 - core) * HALF, HALF), HALF), :]


def sketch_call(place, rows, sketch):
    step = 512
    half = jax.ShapeDtypeStruct((HALF, W), f32)
    return pl.pallas_call(
        sketch_kernel,
        grid=(ROWS // step,),
        out_shape=(half, half),
        in_specs=[
            SMEM,
            pl.BlockSpec((step, W), lambda i: (i, 0)),
            pl.BlockSpec((RANK, W), lambda i: (0, 0)),
        ],
        out_specs=(pl.BlockSpec((HALF, W), lambda i: (0, 0)),) * 2,
        scratch_shapes=[pltpu.VMEM((RANK, W), f32)],
        compiler_params=params(62),
        name="sketch",
    )(place, rows, sketch)


def sum_core_kernel(keep, got, slots, out):
    out[0:HALF, :] = keep[...] + got[...]
    out[HALF:, :] = jnp.zeros((8, W), f32)
    out[HALF:, 0:128] = slots[...]


def sum_first_kernel(r0, r1, r2, r3, out):
    out[0:HALF, :] = (r0[0:HALF, :] + r2[0:HALF, :]) + (r1[0:HALF, :] + r3[0:HALF, :])
    for k, r in enumerate((r0, r1, r2, r3)):
        out[HALF:, k * 128 : (k + 1) * 128] = r[HALF:, 0:128]


def sum_second_kernel(r0, r1, r2, r3, out):
    out[0:HALF, :] = (r0[0:HALF, :] + r2[0:HALF, :]) + (r1[0:HALF, :] + r3[0:HALF, :])
    for k, r in enumerate((r0, r1, r2, r3)):
        out[HALF + 8 * k : HALF + 8 * (k + 1), :] = r[HALF:, :]


def small_call(kernel, rows, name, *args):
    return pl.pallas_call(
        kernel,
        out_shape=jax.ShapeDtypeStruct((rows, W), f32),
        in_specs=[VMEM] * len(args),
        out_specs=VMEM,
        compiler_params=params(),
        name=name,
    )(*args)


def factor_kernel(place, own, other, rows_hbm, out, rows, sem):
    copy = pltpu.make_async_copy(rows_hbm, rows, sem)
    copy.start()
    first = place[1] % 2 == 0
    mine, theirs = own[0:HALF, :], other[0:HALF, :]
    summed = jnp.concatenate(
        [jnp.where(first, mine, theirs), jnp.where(first, theirs, mine)], axis=0
    )
    padded = jnp.concatenate([summed, jnp.zeros((96, W), f32)], axis=0)
    gram = lax.dot_general(
        summed, padded, NT, precision=lax.Precision.HIGHEST, preferred_element_type=f32
    )
    lane = lax.broadcasted_iota(i32, (RANK, 128), 1)
    line = lax.broadcasted_iota(i32, (RANK, 128), 0)
    work = gram + jnp.where(lane == line + RANK, 1.0, 0.0)
    for k in range(RANK - 1):
        column = jnp.broadcast_to(work[:, k : k + 1], (RANK, 128))
        pivot_row = work[k : k + 1, :] / column[k : k + 1, :]
        work = work - jnp.where(line > k, column, 0.0) * pivot_row
    pivots = jnp.sum(jnp.where(lane == line, work, 0.0), axis=1, keepdims=True)
    inverse = work * lax.rsqrt(pivots)
    shifted = jnp.concatenate([jnp.zeros((32, W), f32), summed, jnp.zeros((64, W), f32)], axis=0)
    basis = jnp.dot(
        inverse, shifted, precision=lax.Precision.HIGHEST, preferred_element_type=f32
    ).astype(bf16)
    copy.wait()
    index = lax.broadcasted_iota(i32, (16, BLOCK), 0)
    scales = jnp.zeros((16, BLOCK), f32)
    for b in range(NB_DEV):
        projected = lax.dot_general(
            basis, rows[b * BLOCK : (b + 1) * BLOCK, :], NT, preferred_element_type=f32
        )
        most = jnp.max(jnp.max(jnp.abs(projected), axis=0, keepdims=True), axis=1, keepdims=True)
        scale = (most + 1e-06).astype(bf16).astype(f32)
        factor = (projected / scale).astype(bf16)
        scales = jnp.where(index == b, scale, scales)
        out[b * RANK : (b + 1) * RANK, :] = factor
    out[NB_DEV * RANK :, :] = scales.astype(bf16)


def factor_call(place, own, other, rows):
    return pl.pallas_call(
        factor_kernel,
        out_shape=jax.ShapeDtypeStruct((MSG, BLOCK), bf16),
        in_specs=[SMEM, VMEM, VMEM, ANY],
        out_specs=VMEM,
        scratch_shapes=[pltpu.VMEM((ROWS, W), bf16), pltpu.SemaphoreType.DMA],
        compiler_params=params(),
        name="factor",
    )(place, own, other, rows)


def touch_call(x, us, *after):
    return pl.pallas_call(
        lambda *refs: None,
        out_shape=jax.ShapeDtypeStruct(x.shape, x.dtype),
        in_specs=[ANY] * (1 + len(after)),
        out_specs=ANY,
        input_output_aliases={0: 0},
        compiler_params=params(),
        cost_estimate=pl.CostEstimate(
            flops=0, bytes_accessed=int(us * 3.0e6), transcendentals=0
        ),
        name="touch",
    )(x, *after)


def join_kernel(*refs):
    parts, out, sems = refs[:4], refs[-2], refs[-1]
    copies = [pltpu.make_async_copy(parts[k], out.at[k], sems.at[k]) for k in range(4)]
    for copy in copies:
        copy.start()
    for copy in copies:
        copy.wait()


def join_call(parts, *after):
    return pl.pallas_call(
        join_kernel,
        out_shape=jax.ShapeDtypeStruct((4, MSG, BLOCK), bf16),
        in_specs=[ANY] * (4 + len(after)),
        out_specs=ANY,
        scratch_shapes=[pltpu.SemaphoreType.DMA((4,))],
        compiler_params=params(),
        name="join",
    )(*parts, *after)


def plan_kernel(place, own, other, *refs):
    outs, gathered = refs[:N_SET], refs[N_SET]
    me_set, me = place[0], place[1]
    me_z, me_y, me_core = me // 8, (me // 2) % 4, me % 2
    for core, r in enumerate((own, other)):
        for second in range(4):
            for first in range(4):
                s = (core * 4 + second) * 4 + first
                gathered[s * 8 : (s + 1) * 8, :] = r[
                    HALF + 8 * second : HALF + 8 * (second + 1), first * 128 : (first + 1) * 128
                ]
    fields = jnp.concatenate(
        [gathered[pl.ds(n, N_CAND, stride=8), :] for n in range(8)], axis=0
    ).astype(bf16)
    line = lax.broadcasted_iota(i32, (16, 128), 0)
    lane = lax.broadcasted_iota(i32, (16, 128), 1)
    wanted = ((me_set + line) % N_SET) * N_CAND + me
    hot = jnp.where((lane == wanted) & (line < N_SET), 1.0, 0.0).astype(bf16)
    across = lax.dot_general(hot, fields, NT, preferred_element_type=f32)
    down = lax.dot_general(fields, hot, NT, preferred_element_type=f32)
    n = ENTRIES
    sender = lax.broadcasted_iota(i32, (16, n), 1) % N_CAND
    left = across[:, 0:n] + (sender * NB_DEV - ZERO).astype(f32)
    block = across[:, n : 2 * n].astype(i32)
    owner = block // NB_DEV
    z, y, core = owner // 8, (owner // 2) % 4, owner % 2
    z, y = (z - me_z + 4) % 4, (y - me_y + 4) % 4
    at = jnp.where(core == 0, z * 4 + y, y * 4 + z) + ((core + me_core) % 2) * 16
    right = (at * NB_DEV + block % NB_DEV).astype(f32)
    target = jnp.where(across[:, 3 * n :] != 0, across[:, 2 * n : 3 * n], NT_DEV)
    target_down = jnp.where(down[3 * n :, :] != 0, down[2 * n : 3 * n, :], NT_DEV)
    before = lax.broadcasted_iota(i32, (n, n), 1) < lax.broadcasted_iota(i32, (n, n), 0)
    spots = lax.broadcasted_iota(i32, (n, 128), 1).astype(f32)
    spot = lax.broadcasted_iota(i32, (1, 128), 1)
    line = lax.broadcasted_iota(i32, (8, 128), 0)
    row = lax.broadcasted_iota(i32, (16, n), 0)
    for gr in range(N_SET):
        t_down, t_across = target_down[:, gr : gr + 1], target[gr : gr + 1, :]
        rank = jnp.sum(
            jnp.where((t_down == t_across) & before, 1.0, 0.0), axis=1, keepdims=True
        )
        count = jnp.sum(jnp.where(t_down == spots, 1.0, 0.0), axis=0, keepdims=True)
        chunks = (count.astype(i32) + (PER_CHUNK - 1)) // PER_CHUNK
        chunks = jnp.where(spot < NT_DEV, chunks, 0).astype(f32)
        start = jnp.sum(jnp.where(spots < t_down, chunks, 0.0), axis=1, keepdims=True)
        place_of = jnp.where(t_down < NT_DEV, start * PER_CHUNK + rank, 1000.0)
        chosen = jnp.where(place_of == spots, 1.0, 0.0).astype(bf16)
        both = jnp.where(
            row == 0, left[gr : gr + 1, :], jnp.where(row == 1, right[gr : gr + 1, :], 0.0)
        ).astype(bf16)
        lists = jnp.dot(both, chosen, preferred_element_type=f32)[0:8, :]
        lists = jnp.where(line == 0, lists + ZERO, jnp.where(line == 2, chunks, lists))
        outs[gr][...] = lists.astype(i32)


def plan_call(place, own, other, *after):
    return pl.pallas_call(
        lambda *refs: plan_kernel(*refs[:3], *refs[3 + len(after) :]),
        out_shape=(jax.ShapeDtypeStruct((8, 128), i32),) * N_SET,
        in_specs=[SMEM, VMEM, VMEM] + [ANY] * len(after),
        out_specs=(VMEM,) * N_SET,
        scratch_shapes=[pltpu.VMEM((N_CAND * 8, 128), f32)],
        compiler_params=params(),
        name="plan",
    )(place, own, other, *after)


def collect(pieces, factors, scales, sems):
    copies = [
        pltpu.make_async_copy(piece, factors.at[pl.ds(4 * n, 4)], sems.at[n])
        for n, piece in enumerate(pieces)
    ]
    for copy in copies:
        copy.start()
    for copy in copies:
        copy.wait()
    for p in range(N_CAND):
        scales[p * NB_DEV : (p + 1) * NB_DEV, :] = factors[p, NB_DEV * RANK :, 0:128].astype(f32)[
            0:NB_DEV, :
        ]
    scales[ZERO : ZERO + 8, :] = jnp.zeros((8, 128), f32)


def block_at(factors, b):
    at = pl.multiple_of((b % NB_DEV) * RANK, RANK)
    return factors.at[(b // NB_DEV) % N_CAND, pl.ds(at, RANK), :]


def expand(pairs, t, factors, scales, lefts, rights, start, total):
    def chunk(q, carry):
        for k in range(PER_CHUNK):
            spot = start + q * PER_CHUNK + k
            left, right = pairs[0, spot], pairs[1, spot]
            weight = scales[pl.ds(left, 1), :] * scales[pl.ds(right, 1), :]
            weight = weight.astype(bf16).astype(f32)
            weight = jnp.concatenate([weight, weight], axis=1)
            here = slice(k * RANK, (k + 1) * RANK)
            lefts[here, :] = (block_at(factors, left)[...].astype(f32) * weight).astype(bf16)
            rights[here, :] = block_at(factors, right)[...]
        total[...] += lax.dot_general(lefts[...], rights[...], TN, preferred_element_type=f32)
        return carry

    total[...] = jnp.zeros_like(total)
    chunks = pairs[2, t]
    lax.fori_loop(0, chunks, chunk, 0)
    return start + chunks * PER_CHUNK


WORK = [
    pltpu.VMEM((N_CAND, MSG, BLOCK), bf16),
    pltpu.VMEM((ZERO + 8, 128), f32),
    pltpu.VMEM((RANK * PER_CHUNK, BLOCK), bf16),
    pltpu.VMEM((RANK * PER_CHUNK, BLOCK), bf16),
    pltpu.VMEM((BLOCK, BLOCK), f32),
    pltpu.SemaphoreType.DMA((8,)),
]


def send_call(next_list, last_list, pieces, cuts):
    n = len(cuts) - 1

    def kernel(next_list, last_list, *refs):
        pieces, outs, work = refs[:8], refs[8 : 8 + 2 * n], refs[8 + 2 * n :]
        factors, scales, lefts, rights, total, sems = work
        collect(pieces, factors, scales, sems)
        for side, pairs in enumerate((next_list, last_list)):
            start = 0
            for t in range(cuts[0]):
                start = start + pairs[2, t] * PER_CHUNK
            for part in range(n):
                for t in range(cuts[part], cuts[part + 1]):
                    start = expand(pairs, t, factors, scales, lefts, rights, start, total)
                    outs[2 * part + side][t - cuts[part]] = total[...].astype(bf16)

    shapes = [
        jax.ShapeDtypeStruct((cuts[part + 1] - cuts[part], BLOCK, BLOCK), bf16)
        for part in range(n)
        for side in range(2)
    ]
    return pl.pallas_call(
        kernel,
        out_shape=shapes,
        in_specs=[SMEM, SMEM] + [ANY] * 8,
        out_specs=[VMEM] * (2 * n),
        scratch_shapes=WORK,
        compiler_params=params(),
        name="send_pairs",
    )(next_list, last_list, *pieces)


def keep_call(pairs, base, pieces, *after):
    def kernel(pairs, base, *refs):
        pieces, (out, *work) = refs[:8], refs[8 + len(after) :]
        factors, scales, lefts, rights, total, sems = work
        collect(pieces, factors, scales, sems)
        start = 0
        for t in range(NT_DEV):
            start = expand(pairs, t, factors, scales, lefts, rights, start, total)
            out[t] = base[t] - total[...]

    return pl.pallas_call(
        kernel,
        out_shape=jax.ShapeDtypeStruct((NT_DEV, BLOCK, BLOCK), f32),
        in_specs=[SMEM, VMEM] + [ANY] * (8 + len(after)),
        out_specs=VMEM,
        scratch_shapes=WORK,
        compiler_params=params(),
        name="keep_pairs",
    )(pairs, base, *pieces, *after)


def final_call(base, parts, cuts):
    def kernel(base, *refs):
        parts, out, sems = refs[: len(parts_in)], refs[-2], refs[-1]
        copies = []
        for n in range(len(cuts) - 1):
            one, two = parts[2 * n], parts[2 * n + 1]
            for t in range(cuts[n], cuts[n + 1]):
                k = t - cuts[n]
                base[t] = base[t] - (one[k].astype(f32) + two[k].astype(f32))
                copy = pltpu.make_async_copy(base.at[t], out.at[t], sems.at[t])
                copy.start()
                copies.append(copy)
        for copy in copies:
            copy.wait()

    parts_in = parts
    return pl.pallas_call(
        kernel,
        out_shape=jax.ShapeDtypeStruct((NT_DEV, BLOCK, BLOCK), f32),
        in_specs=[VMEM] * (1 + len(parts)),
        out_specs=ANY,
        scratch_shapes=[pltpu.SemaphoreType.DMA((NT_DEV,))],
        compiler_params=params(),
        name="final",
    )(base, *parts)


def per_device(panel_rows, sketch, accumulator, left_block, right_block, target_slot, slot_valid):
    rows = panel_rows[0]
    place = jnp.stack([lax.axis_index("set"), lax.axis_index("cand")]).astype(i32)

    keep, give = sketch_call(place, rows, sketch[0].T)
    got = from_core(give)
    slots = jnp.concatenate(
        [x[0, 0].T for x in (left_block, right_block, target_slot, slot_valid)], axis=0
    ).astype(f32)
    part = small_call(sum_core_kernel, HALF + 8, "sum_core", keep, got, slots)
    part = small_call(
        sum_first_kernel, HALF + 8, "sum_first", part, *[from_cand(part, 0, k) for k in (1, 2, 3)]
    )
    own = small_call(
        sum_second_kernel, HALF + 32, "sum_second", part, *[from_cand(part, 1, k) for k in (1, 2, 3)]
    )
    other = from_core(own)

    mine = factor_call(place, own, other, rows)
    line = join_call([mine] + [from_cand(mine, 0, k) for k in (1, 2, 3)])
    here = [line] + [from_cand(line, 1, k) for k in (1, 2, 3)]
    pieces = here + [from_core(x) for x in here]

    far_line = join_call([from_cand(mine, 0, k, far=True) for k in range(4)])
    own_list, next_list, far_list, last_list = plan_call(place, own, other, line)
    far_list = from_set(far_list, 2)

    cuts = (0, 8)
    to_next, to_last = send_call(next_list, last_list, pieces, cuts)
    arrived = [touch_call(x, LAST_US) for x in (from_set(to_next, 3), from_set(to_last, 1))]

    far_here = [far_line] + [from_cand(far_line, 1, k) for k in (1, 2, 3)]
    far_pieces = far_here + [from_core(x) for x in far_here]
    base = keep_call(own_list, accumulator[0], pieces, to_next)
    base = keep_call(far_list, base, far_pieces)
    base = final_call(base, arrived, cuts)
    return base[None]


def solution(mesh):
    placed = (
        P("set", "cand", None),
        P("set", None, None),
        P("set", "cand", None, None),
        P("set", "cand", None, None),
        P("set", "cand", None, None),
        P("set", "cand", None, None),
        P("set", "cand", None, None),
    )
    return jax.shard_map(
        per_device,
        mesh=mesh,
        in_specs=placed,
        out_specs=P("set", "cand", None, None),
        check_vma=False,
    )
```

```python
import jax
import jax.numpy as jnp
from jax import lax
from jax.experimental import pallas as pl
from jax.experimental.pallas import tpu as pltpu
from jax.sharding import PartitionSpec as P

W = 512
RANK = 32
BLOCK = 256
NB_DEV = 8
NT_DEV = 8
N_SET = 4
N_CAND = 32
HALF = RANK // 2
ROWS = NB_DEV * BLOCK
MSG = NB_DEV * RANK + 16
SLOTS = 2
SKETCH_STEPS = 4
PER_CHUNK = 8
ENTRIES = N_CAND * SLOTS
ZERO = NB_DEV * N_CAND
LAST_US = 0
f32, bf16, i32 = jnp.float32, jnp.bfloat16, jnp.int32
VMEM = pl.BlockSpec(memory_space=pltpu.VMEM)
SMEM = pl.BlockSpec(memory_space=pltpu.SMEM)
ANY = pl.BlockSpec(memory_space=pl.ANY)
HBM = pl.BlockSpec(memory_space=pltpu.HBM)
NT = (((1,), (1,)), ((), ()))
TN = (((0,), (0,)), ((), ()))


def params(mib=40):
    return pltpu.CompilerParams(vmem_limit_bytes=mib * 1024 * 1024)


def from_cand(x, leg, k, far=False):
    pairs = []
    for me in range(N_CAND):
        z, y, core = me // 8, (me // 2) % 4, me % 2
        if leg == core:
            y = (y + k) % 4
        else:
            z = (z + k) % 4
        pairs.append((z * 8 + y * 2 + core, me))
    if not far:
        return lax.ppermute(x, "cand", pairs)
    pairs = [
        ((me_set + 2) % N_SET * N_CAND + source, me_set * N_CAND + me)
        for me_set in range(N_SET)
        for source, me in pairs
    ]
    return lax.ppermute(x, ("set", "cand"), pairs)


def from_core(x):
    return lax.ppermute(x, "cand", [(me ^ 1, me) for me in range(N_CAND)])


def from_set(x, d):
    return lax.ppermute(x, "set", [((me + d) % N_SET, me) for me in range(N_SET)])


def sketch_kernel(place, rows_hbm, sketch, keep, give, rows, total, sems):
    copies = []
    for n in range(SKETCH_STEPS):
        part = pl.ds(n * (ROWS // SKETCH_STEPS), ROWS // SKETCH_STEPS)
        copies.append(pltpu.make_async_copy(rows_hbm.at[part], rows.at[part], sems.at[n]))
        copies[n].start()
    summed = jnp.zeros((RANK, W), f32)
    for n in range(SKETCH_STEPS):
        copies[n].wait()
        part = rows[n * (ROWS // SKETCH_STEPS) : (n + 1) * (ROWS // SKETCH_STEPS), :]
        sketched = lax.dot_general(sketch[...], part, NT, preferred_element_type=f32)
        summed += jnp.dot(sketched.astype(bf16), part, preferred_element_type=f32)
    total[...] = summed
    core = place[1] % 2
    keep[...] = total[pl.ds(pl.multiple_of(core * HALF, HALF), HALF), :]
    give[...] = total[pl.ds(pl.multiple_of((1 - core) * HALF, HALF), HALF), :]


def sketch_call(place, rows, sketch):
    half = jax.ShapeDtypeStruct((HALF, W), f32)
    return pl.pallas_call(
        sketch_kernel,
        out_shape=(half, half),
        in_specs=[SMEM, HBM, VMEM],
        out_specs=(VMEM, VMEM),
        scratch_shapes=[
            pltpu.VMEM((ROWS, W), bf16),
            pltpu.VMEM((RANK, W), f32),
            pltpu.SemaphoreType.DMA((SKETCH_STEPS,)),
        ],
        compiler_params=params(52),
        name="sketch",
    )(place, rows, sketch)


def sum_core_kernel(keep, got, slots, out):
    out[0:HALF, :] = keep[...] + got[...]
    out[HALF:, :] = jnp.zeros((8, W), f32)
    out[HALF:, 0:128] = slots[...]


def sum_first_kernel(r0, r1, r2, r3, out):
    out[0:HALF, :] = (r0[0:HALF, :] + r2[0:HALF, :]) + (r1[0:HALF, :] + r3[0:HALF, :])
    for k, r in enumerate((r0, r1, r2, r3)):
        out[HALF:, k * 128 : (k + 1) * 128] = r[HALF:, 0:128]


def sum_second_kernel(r0, r1, r2, r3, out):
    out[0:HALF, :] = (r0[0:HALF, :] + r2[0:HALF, :]) + (r1[0:HALF, :] + r3[0:HALF, :])
    for k, r in enumerate((r0, r1, r2, r3)):
        out[HALF + 8 * k : HALF + 8 * (k + 1), :] = r[HALF:, :]


def small_call(kernel, rows, name, *args):
    return pl.pallas_call(
        kernel,
        out_shape=jax.ShapeDtypeStruct((rows, W), f32),
        in_specs=[VMEM] * len(args),
        out_specs=VMEM,
        compiler_params=params(),
        name=name,
    )(*args)


def factor_kernel(place, own, other, rows_hbm, out, rows, sem):
    copy = pltpu.make_async_copy(rows_hbm, rows, sem)
    copy.start()
    first = place[1] % 2 == 0
    mine, theirs = own[0:HALF, :], other[0:HALF, :]
    summed = jnp.concatenate(
        [jnp.where(first, mine, theirs), jnp.where(first, theirs, mine)], axis=0
    )
    padded = jnp.concatenate([summed, jnp.zeros((96, W), f32)], axis=0)
    gram = lax.dot_general(
        summed, padded, NT, precision=lax.Precision.HIGHEST, preferred_element_type=f32
    )
    lane = lax.broadcasted_iota(i32, (RANK, 128), 1)
    line = lax.broadcasted_iota(i32, (RANK, 128), 0)
    work = gram + jnp.where(lane == line + RANK, 1.0, 0.0)
    for k in range(RANK - 1):
        column = jnp.broadcast_to(work[:, k : k + 1], (RANK, 128))
        pivot_row = work[k : k + 1, :] / column[k : k + 1, :]
        work = work - jnp.where(line > k, column, 0.0) * pivot_row
    pivots = jnp.sum(jnp.where(lane == line, work, 0.0), axis=1, keepdims=True)
    inverse = work * lax.rsqrt(pivots)
    shifted = jnp.concatenate([jnp.zeros((32, W), f32), summed, jnp.zeros((64, W), f32)], axis=0)
    basis = jnp.dot(
        inverse, shifted, precision=lax.Precision.HIGHEST, preferred_element_type=f32
    ).astype(bf16)
    copy.wait()
    index = lax.broadcasted_iota(i32, (16, BLOCK), 0)
    scales = jnp.zeros((16, BLOCK), f32)
    for b in range(NB_DEV):
        projected = lax.dot_general(
            basis, rows[b * BLOCK : (b + 1) * BLOCK, :], NT, preferred_element_type=f32
        )
        most = jnp.max(jnp.max(jnp.abs(projected), axis=0, keepdims=True), axis=1, keepdims=True)
        scale = (most + 1e-06).astype(bf16).astype(f32)
        factor = (projected / scale).astype(bf16)
        scales = jnp.where(index == b, scale, scales)
        out[b * RANK : (b + 1) * RANK, :] = factor
    out[NB_DEV * RANK :, :] = scales.astype(bf16)


def factor_call(place, own, other, rows):
    return pl.pallas_call(
        factor_kernel,
        out_shape=jax.ShapeDtypeStruct((MSG, BLOCK), bf16),
        in_specs=[SMEM, VMEM, VMEM, HBM],
        out_specs=VMEM,
        scratch_shapes=[pltpu.VMEM((ROWS, W), bf16), pltpu.SemaphoreType.DMA],
        compiler_params=params(52),
        name="factor",
    )(place, own, other, rows)


def touch_call(x, us, *after):
    return pl.pallas_call(
        lambda *refs: None,
        out_shape=jax.ShapeDtypeStruct(x.shape, x.dtype),
        in_specs=[ANY] * (1 + len(after)),
        out_specs=ANY,
        input_output_aliases={0: 0},
        compiler_params=params(),
        cost_estimate=pl.CostEstimate(
            flops=0, bytes_accessed=int(us * 3.0e6), transcendentals=0
        ),
        name="touch",
    )(x, *after)


def join_kernel(*refs):
    for k in range(4):
        refs[-1][k * MSG : (k + 1) * MSG, :] = refs[k][...]


def join_call(parts, *after):
    return pl.pallas_call(
        join_kernel,
        out_shape=jax.ShapeDtypeStruct((4 * MSG, BLOCK), bf16),
        in_specs=[VMEM] * 4 + [ANY] * len(after),
        out_specs=VMEM,
        compiler_params=params(),
        name="join",
    )(*parts, *after)


def put_call(whole, part, n):
    def kernel(*refs):
        out, sem = refs[-2:]
        copy = pltpu.make_async_copy(refs[-3], out.at[pl.ds(n * 4 * MSG, 4 * MSG)], sem)
        copy.start()
        copy.wait()

    first = whole is None
    return pl.pallas_call(
        kernel,
        out_shape=jax.ShapeDtypeStruct((N_CAND * MSG, BLOCK), bf16),
        in_specs=[ANY] * (1 if first else 2),
        out_specs=ANY,
        input_output_aliases={} if first else {0: 0},
        scratch_shapes=[pltpu.SemaphoreType.DMA],
        compiler_params=params(),
        name="put",
    )(*([part] if first else [whole, part]))


def put_all(parts):
    whole = None
    for n, part in parts:
        whole = put_call(whole, part, n)
    return whole


def plan_kernel(place, own, other, *refs):
    outs, gathered = refs[:N_SET], refs[N_SET]
    me_set, me = place[0], place[1]
    me_z, me_y, me_core = me // 8, (me // 2) % 4, me % 2
    for core, r in enumerate((own, other)):
        for second in range(4):
            for first in range(4):
                s = (core * 4 + second) * 4 + first
                gathered[s * 8 : (s + 1) * 8, :] = r[
                    HALF + 8 * second : HALF + 8 * (second + 1), first * 128 : (first + 1) * 128
                ]
    fields = jnp.concatenate(
        [gathered[pl.ds(n, N_CAND, stride=8), :] for n in range(8)], axis=0
    ).astype(bf16)
    line = lax.broadcasted_iota(i32, (16, 128), 0)
    lane = lax.broadcasted_iota(i32, (16, 128), 1)
    wanted = ((me_set + line) % N_SET) * N_CAND + me
    hot = jnp.where((lane == wanted) & (line < N_SET), 1.0, 0.0).astype(bf16)
    across = lax.dot_general(hot, fields, NT, preferred_element_type=f32)
    down = lax.dot_general(fields, hot, NT, preferred_element_type=f32)
    n = ENTRIES
    sender = lax.broadcasted_iota(i32, (16, n), 1) % N_CAND
    left = across[:, 0:n] + (sender * NB_DEV - ZERO).astype(f32)
    block = across[:, n : 2 * n].astype(i32)
    owner = block // NB_DEV
    z, y, core = owner // 8, (owner // 2) % 4, owner % 2
    z, y = (z - me_z + 4) % 4, (y - me_y + 4) % 4
    at = jnp.where(core == 0, z * 4 + y, y * 4 + z) + ((core + me_core) % 2) * 16
    right = (at * NB_DEV + block % NB_DEV).astype(f32)
    target = jnp.where(across[:, 3 * n :] != 0, across[:, 2 * n : 3 * n], NT_DEV)
    target_down = jnp.where(down[3 * n :, :] != 0, down[2 * n : 3 * n, :], NT_DEV)
    before = lax.broadcasted_iota(i32, (n, n), 1) < lax.broadcasted_iota(i32, (n, n), 0)
    spots = lax.broadcasted_iota(i32, (n, 128), 1).astype(f32)
    spot = lax.broadcasted_iota(i32, (1, 128), 1)
    line = lax.broadcasted_iota(i32, (8, 128), 0)
    lane = lax.broadcasted_iota(i32, (8, 128), 1)
    row = lax.broadcasted_iota(i32, (16, n), 0)
    for gr in range(N_SET):
        t_down, t_across = target_down[:, gr : gr + 1], target[gr : gr + 1, :]
        rank = jnp.sum(
            jnp.where((t_down == t_across) & before, 1.0, 0.0), axis=1, keepdims=True
        )
        count = jnp.sum(jnp.where(t_down == spots, 1.0, 0.0), axis=0, keepdims=True)
        chunks = (count.astype(i32) + (PER_CHUNK - 1)) // PER_CHUNK
        chunks = jnp.where(spot < NT_DEV, chunks, 0).astype(f32)
        start = jnp.sum(jnp.where(spots < t_down, chunks, 0.0), axis=1, keepdims=True)
        end = jnp.sum(jnp.where(lane <= line, chunks, 0.0), axis=1, keepdims=True)
        target_of = jnp.sum(jnp.where(end <= lane.astype(f32), 1.0, 0.0), axis=0, keepdims=True)
        target_of = jnp.minimum(target_of, NT_DEV - 1)
        pieces = jnp.sum(chunks, axis=1, keepdims=True)
        place_of = jnp.where(t_down < NT_DEV, start * PER_CHUNK + rank, 1000.0)
        chosen = jnp.where(place_of == spots, 1.0, 0.0).astype(bf16)
        both = jnp.where(
            row == 0, left[gr : gr + 1, :], jnp.where(row == 1, right[gr : gr + 1, :], 0.0)
        ).astype(bf16)
        lists = jnp.dot(both, chosen, preferred_element_type=f32)[0:8, :]
        lists = jnp.where(line == 0, lists + ZERO, lists)
        lists = jnp.where(line == 2, target_of, jnp.where(line == 3, pieces, lists))
        lists = lists.astype(i32)
        begins = (lists // NB_DEV) % N_CAND * MSG + lists % NB_DEV * RANK
        outs[gr][0:4, :] = lists[0:4, :]
        outs[gr][4:6, :] = begins[0:2, :]


def plan_call(place, own, other, *after):
    return pl.pallas_call(
        lambda *refs: plan_kernel(*refs[:3], *refs[3 + len(after) :]),
        out_shape=(jax.ShapeDtypeStruct((8, 128), i32),) * N_SET,
        in_specs=[SMEM, VMEM, VMEM] + [ANY] * len(after),
        out_specs=(VMEM,) * N_SET,
        scratch_shapes=[pltpu.VMEM((N_CAND * 8, 128), f32)],
        compiler_params=params(),
        name="plan",
    )(place, own, other, *after)


def spread(factors, scales):
    for p in range(N_CAND):
        rows = factors[p * MSG + NB_DEV * RANK : (p + 1) * MSG, 0:128].astype(f32)
        scales[p * NB_DEV : (p + 1) * NB_DEV, :] = rows[0:NB_DEV, :]
    scales[ZERO : ZERO + 8, :] = jnp.zeros((8, 128), f32)


def block_at(factors, begin):
    return factors[pl.ds(pl.multiple_of(begin, 16), RANK), :]


def expand(pairs, factors, scales, lefts, rights, totals):
    def chunk(q, side):
        for k in range(PER_CHUNK):
            spot = q * PER_CHUNK + k
            left, right = pairs[0, spot], pairs[1, spot]
            weight = scales[pl.ds(left, 1), :] * scales[pl.ds(right, 1), :]
            weight = jnp.broadcast_to(weight, (RANK, 128)).astype(bf16)
            weight = jnp.concatenate([weight, weight], axis=1)
            here = slice(k * RANK, (k + 1) * RANK)
            lefts[side, here, :] = block_at(factors, pairs[4, spot]) * weight
            rights[side, here, :] = block_at(factors, pairs[5, spot])

    def couple(n, carry):
        chunk(2 * n, 0)
        chunk(2 * n + 1, 1)
        terms = [
            lax.dot_general(lefts[side], rights[side], TN, preferred_element_type=f32)
            for side in range(2)
        ]
        for side in range(2):
            t = pairs[2, 2 * n + side]
            totals[t] += terms[side]
        return carry

    totals[...] = jnp.zeros_like(totals)
    lax.fori_loop(0, (pairs[3, 0] + 1) // 2, couple, 0)


WORK = [
    pltpu.VMEM((ZERO + 8, 128), f32),
    pltpu.VMEM((2, RANK * PER_CHUNK, BLOCK), bf16),
    pltpu.VMEM((2, RANK * PER_CHUNK, BLOCK), bf16),
    pltpu.VMEM((NT_DEV, BLOCK, BLOCK), f32),
]


def send_call(next_list, last_list, factors):
    def kernel(next_list, last_list, factors, to_next, to_last, scales, lefts, rights, totals):
        spread(factors, scales)
        for pairs, out in ((next_list, to_next), (last_list, to_last)):
            expand(pairs, factors, scales, lefts, rights, totals)
            out[...] = totals[...].astype(bf16)

    out = jax.ShapeDtypeStruct((NT_DEV, BLOCK, BLOCK), bf16)
    return pl.pallas_call(
        kernel,
        out_shape=(out, out),
        in_specs=[SMEM, SMEM, VMEM],
        out_specs=(VMEM, VMEM),
        scratch_shapes=WORK,
        compiler_params=params(),
        name="send_pairs",
    )(next_list, last_list, factors)


def keep_call(pairs, base, factors, *after):
    def kernel(pairs, base, factors, *refs):
        out, scales, lefts, rights, totals = refs[len(after) :]
        spread(factors, scales)
        expand(pairs, factors, scales, lefts, rights, totals)
        out[...] = base[...] - totals[...]

    return pl.pallas_call(
        kernel,
        out_shape=jax.ShapeDtypeStruct((NT_DEV, BLOCK, BLOCK), f32),
        in_specs=[SMEM, VMEM, VMEM] + [ANY] * len(after),
        out_specs=VMEM,
        scratch_shapes=WORK,
        compiler_params=params(),
        name="keep_pairs",
    )(pairs, base, factors, *after)


def final_call(base, one, two):
    def kernel(base, one, two, out, sems):
        copies = []
        for t in range(NT_DEV):
            base[t] = base[t] - (one[t].astype(f32) + two[t].astype(f32))
            copies.append(pltpu.make_async_copy(base.at[t], out.at[t], sems.at[t]))
            copies[t].start()
        for copy in copies:
            copy.wait()

    return pl.pallas_call(
        kernel,
        out_shape=jax.ShapeDtypeStruct((NT_DEV, BLOCK, BLOCK), f32),
        in_specs=[VMEM] * 3,
        out_specs=ANY,
        scratch_shapes=[pltpu.SemaphoreType.DMA((NT_DEV,))],
        compiler_params=params(),
        name="final",
    )(base, one, two)


def per_device(panel_rows, sketch, accumulator, left_block, right_block, target_slot, slot_valid):
    rows = panel_rows[0]
    place = jnp.stack([lax.axis_index("set"), lax.axis_index("cand")]).astype(i32)

    keep, give = sketch_call(place, rows, sketch[0].T)
    got = from_core(give)
    slots = jnp.concatenate(
        [x[0, 0].T for x in (left_block, right_block, target_slot, slot_valid)], axis=0
    ).astype(f32)
    part = small_call(sum_core_kernel, HALF + 8, "sum_core", keep, got, slots)
    part = small_call(
        sum_first_kernel, HALF + 8, "sum_first", part, *[from_cand(part, 0, k) for k in (1, 2, 3)]
    )
    own = small_call(
        sum_second_kernel, HALF + 32, "sum_second", part, *[from_cand(part, 1, k) for k in (1, 2, 3)]
    )
    other = from_core(own)

    mine = factor_call(place, own, other, rows)
    far = from_set(mine, 2)
    parts = [mine] + [from_cand(mine, 0, k) for k in (1, 2, 3)]
    line = join_call(parts)
    opposite = from_cand(line, 1, 2)
    far_line = join_call([far] + [from_cand(far, 0, k) for k in (1, 2, 3)])
    own_list, next_list, far_list, last_list = plan_call(place, own, other, far_line)
    far_list = from_set(far_list, 2)
    line = join_call(parts, far_line)
    opposite = touch_call(opposite, 0, far_list)
    here = [line, from_cand(line, 1, 1), opposite, from_cand(line, 1, 3)]
    there = [from_core(x) for x in here]
    factors = put_all(
        [p for k in range(4) for p in ((k, here[k]), (4 + k, there[k]))]
    )

    to_next, to_last = send_call(next_list, last_list, factors)
    arrived = [touch_call(x, LAST_US) for x in (from_set(to_next, 3), from_set(to_last, 1))]

    far_here = [far_line] + [from_cand(far_line, 1, k) for k in (1, 2, 3)]
    far_there = [from_core(x) for x in far_here]
    far_factors = put_all(
        [p for k in range(4) for p in ((k, far_here[k]), (4 + k, far_there[k]))]
    )
    base = keep_call(own_list, accumulator[0], factors, to_next)
    base = keep_call(far_list, base, far_factors)
    base = final_call(base, *arrived)
    return base[None]


def solution(mesh):
    placed = (
        P("set", "cand", None),
        P("set", None, None),
        P("set", "cand", None, None),
        P("set", "cand", None, None),
        P("set", "cand", None, None),
        P("set", "cand", None, None),
        P("set", "cand", None, None),
    )
    return jax.shard_map(
        per_device,
        mesh=mesh,
        in_specs=placed,
        out_specs=P("set", "cand", None, None),
        check_vma=False,
    )
```

```python
import jax
import jax.numpy as jnp
from jax import lax
from jax.experimental import pallas as pl
from jax.experimental.pallas import tpu as pltpu
from jax.sharding import PartitionSpec as P

W = 512
RANK = 32
BLOCK = 256
NB_DEV = 8
NT_DEV = 8
N_SET = 4
N_CAND = 32
HALF = RANK // 2
ROWS = NB_DEV * BLOCK
MSG = NB_DEV * RANK + 16
SLOTS = 2
SKETCH_STEPS = 4
PER_CHUNK = 8
ENTRIES = N_CAND * SLOTS
ZERO = NB_DEV * N_CAND
LAST_US = 0
f32, bf16, i32 = jnp.float32, jnp.bfloat16, jnp.int32
VMEM = pl.BlockSpec(memory_space=pltpu.VMEM)
SMEM = pl.BlockSpec(memory_space=pltpu.SMEM)
ANY = pl.BlockSpec(memory_space=pl.ANY)
HBM = pl.BlockSpec(memory_space=pltpu.HBM)
NT = (((1,), (1,)), ((), ()))
TN = (((0,), (0,)), ((), ()))


def params(mib=40):
    return pltpu.CompilerParams(vmem_limit_bytes=mib * 1024 * 1024)


def from_cand(x, leg, k):
    pairs = []
    for me in range(N_CAND):
        z, y, core = me // 8, (me // 2) % 4, me % 2
        if leg == core:
            y = (y + k) % 4
        else:
            z = (z + k) % 4
        pairs.append((z * 8 + y * 2 + core, me))
    return lax.ppermute(x, "cand", pairs)


def from_core(x):
    return lax.ppermute(x, "cand", [(me ^ 1, me) for me in range(N_CAND)])


def from_set(x, d):
    return lax.ppermute(x, "set", [((me + d) % N_SET, me) for me in range(N_SET)])


def sketch_kernel(place, rows_hbm, sketch, keep, give, rows, total, sems):
    copies = []
    for n in range(SKETCH_STEPS):
        part = pl.ds(n * (ROWS // SKETCH_STEPS), ROWS // SKETCH_STEPS)
        copies.append(pltpu.make_async_copy(rows_hbm.at[part], rows.at[part], sems.at[n]))
        copies[n].start()
    summed = jnp.zeros((RANK, W), f32)
    for n in range(SKETCH_STEPS):
        copies[n].wait()
        part = rows[n * (ROWS // SKETCH_STEPS) : (n + 1) * (ROWS // SKETCH_STEPS), :]
        sketched = lax.dot_general(sketch[...], part, NT, preferred_element_type=f32)
        summed += jnp.dot(sketched.astype(bf16), part, preferred_element_type=f32)
    total[...] = summed
    core = place[1] % 2
    keep[...] = total[pl.ds(pl.multiple_of(core * HALF, HALF), HALF), :]
    give[...] = total[pl.ds(pl.multiple_of((1 - core) * HALF, HALF), HALF), :]


def sketch_call(place, rows, sketch):
    half = jax.ShapeDtypeStruct((HALF, W), f32)
    return pl.pallas_call(
        sketch_kernel,
        out_shape=(half, half),
        in_specs=[SMEM, HBM, VMEM],
        out_specs=(VMEM, VMEM),
        scratch_shapes=[
            pltpu.VMEM((ROWS, W), bf16),
            pltpu.VMEM((RANK, W), f32),
            pltpu.SemaphoreType.DMA((SKETCH_STEPS,)),
        ],
        compiler_params=params(52),
        name="sketch",
    )(place, rows, sketch)


def sum_core_kernel(keep, got, slots, out):
    out[0:HALF, :] = keep[...] + got[...]
    out[HALF:, :] = jnp.zeros((8, W), f32)
    out[HALF:, 0:128] = slots[...]


def sum_first_kernel(r0, r1, r2, r3, out):
    out[0:HALF, :] = (r0[0:HALF, :] + r2[0:HALF, :]) + (r1[0:HALF, :] + r3[0:HALF, :])
    for k, r in enumerate((r0, r1, r2, r3)):
        out[HALF:, k * 128 : (k + 1) * 128] = r[HALF:, 0:128]


def sum_second_kernel(r0, r1, r2, r3, out):
    out[0:HALF, :] = (r0[0:HALF, :] + r2[0:HALF, :]) + (r1[0:HALF, :] + r3[0:HALF, :])
    for k, r in enumerate((r0, r1, r2, r3)):
        out[HALF + 8 * k : HALF + 8 * (k + 1), :] = r[HALF:, :]


def small_call(kernel, rows, name, *args):
    return pl.pallas_call(
        kernel,
        out_shape=jax.ShapeDtypeStruct((rows, W), f32),
        in_specs=[VMEM] * len(args),
        out_specs=VMEM,
        compiler_params=params(),
        name=name,
    )(*args)


def factor_kernel(place, own, other, rows_hbm, out, rows, sem):
    copy = pltpu.make_async_copy(rows_hbm, rows, sem)
    copy.start()
    first = place[1] % 2 == 0
    mine, theirs = own[0:HALF, :], other[0:HALF, :]
    summed = jnp.concatenate(
        [jnp.where(first, mine, theirs), jnp.where(first, theirs, mine)], axis=0
    )
    padded = jnp.concatenate([summed, jnp.zeros((96, W), f32)], axis=0)
    gram = lax.dot_general(
        summed, padded, NT, precision=lax.Precision.HIGHEST, preferred_element_type=f32
    )
    lane = lax.broadcasted_iota(i32, (RANK, 128), 1)
    line = lax.broadcasted_iota(i32, (RANK, 128), 0)
    work = gram + jnp.where(lane == line + RANK, 1.0, 0.0)
    for k in range(0, RANK, 2):
        first_column = jnp.broadcast_to(work[:, k : k + 1], (RANK, 128))
        second_column = jnp.broadcast_to(work[:, k + 1 : k + 2], (RANK, 128))
        inverse = 1.0 / first_column[k : k + 1, :]
        first_row = work[k : k + 1, :] * inverse
        second_column = second_column - first_column * (second_column[k : k + 1, :] * inverse)
        second_row = work[k + 1 : k + 2, :] - first_column[k + 1 : k + 2, :] * first_row
        second_row = second_row / second_column[k + 1 : k + 2, :]
        work = work - (
            jnp.where(line > k, first_column, 0.0) * first_row
            + jnp.where(line > k + 1, second_column, 0.0) * second_row
        )
    pivots = jnp.sum(jnp.where(lane == line, work, 0.0), axis=1, keepdims=True)
    inverse = work * lax.rsqrt(pivots)
    shifted = jnp.concatenate([jnp.zeros((32, W), f32), summed, jnp.zeros((64, W), f32)], axis=0)
    basis = jnp.dot(
        inverse, shifted, precision=lax.Precision.HIGHEST, preferred_element_type=f32
    ).astype(bf16)
    copy.wait()
    index = lax.broadcasted_iota(i32, (16, BLOCK), 0)
    scales = jnp.zeros((16, BLOCK), f32)
    for b in range(NB_DEV):
        projected = lax.dot_general(
            basis, rows[b * BLOCK : (b + 1) * BLOCK, :], NT, preferred_element_type=f32
        )
        most = jnp.max(jnp.max(jnp.abs(projected), axis=0, keepdims=True), axis=1, keepdims=True)
        scale = (most + 1e-06).astype(bf16).astype(f32)
        factor = (projected / scale).astype(bf16)
        scales = jnp.where(index == b, scale, scales)
        out[b * RANK : (b + 1) * RANK, :] = factor
    out[NB_DEV * RANK :, :] = scales.astype(bf16)


def factor_call(place, own, other, rows):
    return pl.pallas_call(
        factor_kernel,
        out_shape=jax.ShapeDtypeStruct((MSG, BLOCK), bf16),
        in_specs=[SMEM, VMEM, VMEM, HBM],
        out_specs=VMEM,
        scratch_shapes=[pltpu.VMEM((ROWS, W), bf16), pltpu.SemaphoreType.DMA],
        compiler_params=params(52),
        name="factor",
    )(place, own, other, rows)


def touch_call(x, us, *after):
    return pl.pallas_call(
        lambda *refs: None,
        out_shape=jax.ShapeDtypeStruct(x.shape, x.dtype),
        in_specs=[ANY] * (1 + len(after)),
        out_specs=ANY,
        input_output_aliases={0: 0},
        compiler_params=params(),
        cost_estimate=pl.CostEstimate(
            flops=0, bytes_accessed=int(us * 3.0e6), transcendentals=0
        ),
        name="touch",
    )(x, *after)


def join_call(parts, name, *after):
    heights = [part.shape[0] for part in parts]

    def kernel(*refs):
        at = 0
        for ref, height in zip(refs, heights):
            refs[-1][at : at + height, :] = ref[...]
            at += height

    return pl.pallas_call(
        kernel,
        out_shape=jax.ShapeDtypeStruct((sum(heights), BLOCK), bf16),
        in_specs=[VMEM] * len(parts) + [ANY] * len(after),
        out_specs=VMEM,
        compiler_params=params(),
        name=name,
    )(*parts, *after)


def put_call(whole, part, n):
    def kernel(*refs):
        out, sem = refs[-2:]
        copy = pltpu.make_async_copy(
            refs[-3].at[pl.ds(0, 4 * MSG)], out.at[pl.ds(n * 4 * MSG, 4 * MSG)], sem
        )
        copy.start()
        copy.wait()

    first = whole is None
    return pl.pallas_call(
        kernel,
        out_shape=jax.ShapeDtypeStruct((N_CAND * MSG, BLOCK), bf16),
        in_specs=[ANY] * (1 if first else 2),
        out_specs=ANY,
        input_output_aliases={} if first else {0: 0},
        scratch_shapes=[pltpu.SemaphoreType.DMA],
        compiler_params=params(),
        name="put",
    )(*([part] if first else [whole, part]))


def put_all(parts):
    whole = None
    for n, part in parts:
        whole = put_call(whole, part, n)
    return whole


def with_begins(lists, out):
    begins = (lists // NB_DEV) % N_CAND * MSG + lists % NB_DEV * RANK
    out[0:4, :] = lists[0:4, :]
    out[4:6, :] = begins[0:2, :]
    out[6:8, :] = lists[6:8, :]


def plan_kernel(place, own, other, *refs):
    outs, gathered = refs[:N_SET], refs[N_SET]
    me_set, me = place[0], place[1]
    me_z, me_y, me_core = me // 8, (me // 2) % 4, me % 2
    for core, r in enumerate((own, other)):
        for second in range(4):
            for first in range(4):
                s = (core * 4 + second) * 4 + first
                gathered[s * 8 : (s + 1) * 8, :] = r[
                    HALF + 8 * second : HALF + 8 * (second + 1), first * 128 : (first + 1) * 128
                ]
    fields = jnp.concatenate(
        [gathered[pl.ds(n, N_CAND, stride=8), :] for n in range(8)], axis=0
    ).astype(bf16)
    line = lax.broadcasted_iota(i32, (16, 128), 0)
    lane = lax.broadcasted_iota(i32, (16, 128), 1)
    wanted = ((me_set + line) % N_SET) * N_CAND + me
    hot = jnp.where((lane == wanted) & (line < N_SET), 1.0, 0.0).astype(bf16)
    across = lax.dot_general(hot, fields, NT, preferred_element_type=f32)
    down = lax.dot_general(fields, hot, NT, preferred_element_type=f32)
    n = ENTRIES
    sender = lax.broadcasted_iota(i32, (16, n), 1) % N_CAND
    left = across[:, 0:n] + (sender * NB_DEV - ZERO).astype(f32)
    block = across[:, n : 2 * n].astype(i32)
    owner = block // NB_DEV
    z, y, core = owner // 8, (owner // 2) % 4, owner % 2
    z, y = (z - me_z + 4) % 4, (y - me_y + 4) % 4
    at = jnp.where(core == 0, z * 4 + y, y * 4 + z) + ((core + me_core) % 2) * 16
    right = (at * NB_DEV + block % NB_DEV).astype(f32)
    target = jnp.where(across[:, 3 * n :] != 0, across[:, 2 * n : 3 * n], NT_DEV)
    target_down = jnp.where(down[3 * n :, :] != 0, down[2 * n : 3 * n, :], NT_DEV)
    before = lax.broadcasted_iota(i32, (n, n), 1) < lax.broadcasted_iota(i32, (n, n), 0)
    spots = lax.broadcasted_iota(i32, (n, 128), 1).astype(f32)
    spot = lax.broadcasted_iota(i32, (1, 128), 1)
    line = lax.broadcasted_iota(i32, (8, 128), 0)
    lane = lax.broadcasted_iota(i32, (8, 128), 1)
    row = lax.broadcasted_iota(i32, (16, n), 0)
    for gr in range(N_SET):
        t_down, t_across = target_down[:, gr : gr + 1], target[gr : gr + 1, :]
        rank = jnp.sum(
            jnp.where((t_down == t_across) & before, 1.0, 0.0), axis=1, keepdims=True
        )
        count = jnp.sum(jnp.where(t_down == spots, 1.0, 0.0), axis=0, keepdims=True)
        chunks = (count.astype(i32) + (PER_CHUNK - 1)) // PER_CHUNK
        chunks = jnp.where(spot < NT_DEV, chunks, 0).astype(f32)
        start = jnp.sum(jnp.where(spots < t_down, chunks, 0.0), axis=1, keepdims=True)
        end = jnp.sum(jnp.where(lane <= line, chunks, 0.0), axis=1, keepdims=True)
        target_of = jnp.sum(jnp.where(end <= lane.astype(f32), 1.0, 0.0), axis=0, keepdims=True)
        target_of = jnp.minimum(target_of, NT_DEV - 1)
        pieces = jnp.sum(chunks, axis=1, keepdims=True)
        place_of = jnp.where(t_down < NT_DEV, start * PER_CHUNK + rank, 1000.0)
        chosen = jnp.where(place_of == spots, 1.0, 0.0).astype(bf16)
        both = jnp.where(
            row == 0, left[gr : gr + 1, :], jnp.where(row == 1, right[gr : gr + 1, :], 0.0)
        ).astype(bf16)
        lists = jnp.dot(both, chosen, preferred_element_type=f32)[0:8, :]
        lists = jnp.where(line == 0, lists + ZERO, lists)
        lists = jnp.where(line == 2, target_of, jnp.where(line == 3, pieces, lists))
        lists = jnp.where(line == 6, chunks, lists)
        if gr == 2:
            lists = jnp.concatenate([lists, jnp.zeros((8, 128), f32)], axis=0).astype(bf16)
            outs[gr][...] = jnp.concatenate([lists, jnp.zeros((16, 128), bf16)], axis=1)
        else:
            with_begins(lists.astype(i32), outs[gr])


def plan_call(place, own, other, *after):
    shapes = [jax.ShapeDtypeStruct((8, 128), i32)] * N_SET
    shapes[2] = jax.ShapeDtypeStruct((16, BLOCK), bf16)
    return pl.pallas_call(
        lambda *refs: plan_kernel(*refs[:3], *refs[3 + len(after) :]),
        out_shape=shapes,
        in_specs=[SMEM, VMEM, VMEM] + [ANY] * len(after),
        out_specs=[VMEM] * N_SET,
        scratch_shapes=[pltpu.VMEM((N_CAND * 8, 128), f32)],
        compiler_params=params(),
        name="plan",
    )(place, own, other, *after)


def unpack_call(message):
    def kernel(message, out):
        lists = message[4 * MSG :, 0:128].astype(f32)[0:8, :]
        with_begins(lists.astype(i32), out)

    return pl.pallas_call(
        kernel,
        out_shape=jax.ShapeDtypeStruct((8, 128), i32),
        in_specs=[VMEM],
        out_specs=VMEM,
        compiler_params=params(),
        name="unpack",
    )(message)


def spread(factors, scales):
    for p in range(N_CAND):
        rows = factors[p * MSG + NB_DEV * RANK : (p + 1) * MSG, 0:128].astype(f32)
        scales[p * NB_DEV : (p + 1) * NB_DEV, :] = rows[0:NB_DEV, :]
    scales[ZERO : ZERO + 8, :] = jnp.zeros((8, 128), f32)


def block_at(factors, begin):
    return factors[pl.ds(pl.multiple_of(begin, 16), RANK), :]


def expand(pairs, factors, scales, lefts, rights, totals):
    def chunk(q, side):
        for k in range(PER_CHUNK):
            spot = q * PER_CHUNK + k
            left, right = pairs[0, spot], pairs[1, spot]
            weight = scales[pl.ds(left, 1), :] * scales[pl.ds(right, 1), :]
            weight = jnp.broadcast_to(weight, (RANK, 128)).astype(bf16)
            weight = jnp.concatenate([weight, weight], axis=1)
            here = slice(k * RANK, (k + 1) * RANK)
            lefts[side, here, :] = block_at(factors, pairs[4, spot]) * weight
            rights[side, here, :] = block_at(factors, pairs[5, spot])

    def couple(n, last):
        chunk(2 * n, 0)
        chunk(2 * n + 1, 1)
        terms = [
            lax.dot_general(lefts[side], rights[side], TN, preferred_element_type=f32)
            for side in range(2)
        ]
        for side in range(2):
            t = pairs[2, 2 * n + side]
            totals[t] = jnp.where(t == last, totals[t], 0.0) + terms[side]
            last = t
        return last

    lax.fori_loop(0, (pairs[3, 0] + 1) // 2, couple, -1)


def total_of(pairs, t, totals):
    return jnp.where(pairs[6, t] > 0, totals[t], 0.0)


WORK = [
    pltpu.VMEM((ZERO + 8, 128), f32),
    pltpu.VMEM((2, RANK * PER_CHUNK, BLOCK), bf16),
    pltpu.VMEM((2, RANK * PER_CHUNK, BLOCK), bf16),
    pltpu.VMEM((NT_DEV, BLOCK, BLOCK), f32),
]


def send_call(next_list, last_list, factors, *after):
    def kernel(next_list, last_list, factors, *refs):
        to_next, to_last, scales, lefts, rights, totals = refs[len(after) :]
        spread(factors, scales)
        for pairs, out in ((next_list, to_next), (last_list, to_last)):
            expand(pairs, factors, scales, lefts, rights, totals)
            for t in range(NT_DEV):
                out[t] = total_of(pairs, t, totals).astype(bf16)

    out = jax.ShapeDtypeStruct((NT_DEV, BLOCK, BLOCK), bf16)
    return pl.pallas_call(
        kernel,
        out_shape=(out, out),
        in_specs=[SMEM, SMEM, VMEM] + [ANY] * len(after),
        out_specs=(VMEM, VMEM),
        scratch_shapes=WORK,
        compiler_params=params(),
        name="send_pairs",
    )(next_list, last_list, factors, *after)


def keep_call(pairs, base, factors, *after):
    def kernel(pairs, base, factors, *refs):
        out, scales, lefts, rights, totals = refs[len(after) :]
        spread(factors, scales)
        expand(pairs, factors, scales, lefts, rights, totals)
        for t in range(NT_DEV):
            out[t] = base[t] - total_of(pairs, t, totals)

    return pl.pallas_call(
        kernel,
        out_shape=jax.ShapeDtypeStruct((NT_DEV, BLOCK, BLOCK), f32),
        in_specs=[SMEM, VMEM, VMEM] + [ANY] * len(after),
        out_specs=VMEM,
        scratch_shapes=WORK,
        compiler_params=params(),
        name="keep_pairs",
    )(pairs, base, factors, *after)


def final_call(base, one, two):
    def kernel(base, one, two, out, sems):
        copies = []
        for t in range(NT_DEV):
            base[t] = base[t] - (one[t].astype(f32) + two[t].astype(f32))
            copies.append(pltpu.make_async_copy(base.at[t], out.at[t], sems.at[t]))
            copies[t].start()
        for copy in copies:
            copy.wait()

    return pl.pallas_call(
        kernel,
        out_shape=jax.ShapeDtypeStruct((NT_DEV, BLOCK, BLOCK), f32),
        in_specs=[VMEM] * 3,
        out_specs=ANY,
        scratch_shapes=[pltpu.SemaphoreType.DMA((NT_DEV,))],
        compiler_params=params(),
        name="final",
    )(base, one, two)


def per_device(panel_rows, sketch, accumulator, left_block, right_block, target_slot, slot_valid):
    rows = panel_rows[0]
    place = jnp.stack([lax.axis_index("set"), lax.axis_index("cand")]).astype(i32)

    keep, give = sketch_call(place, rows, sketch[0].T)
    got = from_core(give)
    slots = jnp.concatenate(
        [x[0, 0].T for x in (left_block, right_block, target_slot, slot_valid)], axis=0
    ).astype(f32)
    part = small_call(sum_core_kernel, HALF + 8, "sum_core", keep, got, slots)
    part = small_call(
        sum_first_kernel, HALF + 8, "sum_first", part, *[from_cand(part, 0, k) for k in (1, 2, 3)]
    )
    own = small_call(
        sum_second_kernel, HALF + 32, "sum_second", part, *[from_cand(part, 1, k) for k in (1, 2, 3)]
    )
    other = from_core(own)

    mine = factor_call(place, own, other, rows)
    own_list, next_list, far_list, last_list = plan_call(place, own, other, mine)
    line = join_call([mine] + [from_cand(mine, 0, k) for k in (1, 2, 3)], "join_line", next_list)
    far_line = from_set(join_call([line, far_list], "join_far"), 2)
    here = [line] + [from_cand(line, 1, k) for k in (1, 2, 3)]
    there = [from_core(x) for x in here]
    factors = put_all(
        [p for k in range(4) for p in ((k, here[k]), (4 + k, there[k]))]
    )

    to_next, to_last = send_call(next_list, last_list, factors)
    arrived = [touch_call(x, LAST_US) for x in (from_set(to_next, 3), from_set(to_last, 1))]

    far_here = [far_line] + [from_cand(far_line, 1, k) for k in (1, 2, 3)]
    far_there = [from_core(x) for x in far_here]
    far_factors = put_all(
        [p for k in range(4) for p in ((k, far_here[k]), (4 + k, far_there[k]))]
    )
    base = keep_call(own_list, accumulator[0], factors, to_next)
    base = keep_call(unpack_call(far_line), base, far_factors)
    base = final_call(base, *arrived)
    return base[None]


def solution(mesh):
    placed = (
        P("set", "cand", None),
        P("set", None, None),
        P("set", "cand", None, None),
        P("set", "cand", None, None),
        P("set", "cand", None, None),
        P("set", "cand", None, None),
        P("set", "cand", None, None),
    )
    return jax.shard_map(
        per_device,
        mesh=mesh,
        in_specs=placed,
        out_specs=P("set", "cand", None, None),
        check_vma=False,
    )
```

```python
import jax
import jax.numpy as jnp
from jax import lax
from jax.experimental import pallas as pl
from jax.experimental.pallas import tpu as pltpu
from jax.sharding import PartitionSpec as P

W = 512
RANK = 32
BLOCK = 256
NB_DEV = 8
NT_DEV = 8
N_SET = 4
N_CAND = 32
HALF = RANK // 2
ROWS = NB_DEV * BLOCK
MSG = NB_DEV * RANK + 16
SLOTS = 2
SKETCH_STEPS = 4
PER_CHUNK = 8
TURN = 4
ENTRIES = N_CAND * SLOTS
ZERO = NB_DEV * N_CAND
LAST_US = 0
f32, bf16, i32 = jnp.float32, jnp.bfloat16, jnp.int32
VMEM = pl.BlockSpec(memory_space=pltpu.VMEM)
SMEM = pl.BlockSpec(memory_space=pltpu.SMEM)
ANY = pl.BlockSpec(memory_space=pl.ANY)
HBM = pl.BlockSpec(memory_space=pltpu.HBM)
NT = (((1,), (1,)), ((), ()))
TN = (((0,), (0,)), ((), ()))


def params(mib=40):
    return pltpu.CompilerParams(vmem_limit_bytes=mib * 1024 * 1024)


def from_cand(x, leg, k):
    pairs = []
    for me in range(N_CAND):
        z, y, core = me // 8, (me // 2) % 4, me % 2
        if leg == core:
            y = (y + k) % 4
        else:
            z = (z + k) % 4
        pairs.append((z * 8 + y * 2 + core, me))
    return lax.ppermute(x, "cand", pairs)


def from_core(x):
    return lax.ppermute(x, "cand", [(me ^ 1, me) for me in range(N_CAND)])


def from_set(x, d):
    return lax.ppermute(x, "set", [((me + d) % N_SET, me) for me in range(N_SET)])


def sketch_kernel(place, rows_hbm, sketch, keep, give, rows, total, sems):
    copies = []
    for n in range(SKETCH_STEPS):
        part = pl.ds(n * (ROWS // SKETCH_STEPS), ROWS // SKETCH_STEPS)
        copies.append(pltpu.make_async_copy(rows_hbm.at[part], rows.at[part], sems.at[n]))
        copies[n].start()
    summed = jnp.zeros((RANK, W), f32)
    for n in range(SKETCH_STEPS):
        copies[n].wait()
        part = rows[n * (ROWS // SKETCH_STEPS) : (n + 1) * (ROWS // SKETCH_STEPS), :]
        sketched = lax.dot_general(sketch[...], part, NT, preferred_element_type=f32)
        summed += jnp.dot(sketched.astype(bf16), part, preferred_element_type=f32)
    total[...] = summed
    core = place[1] % 2
    keep[...] = total[pl.ds(pl.multiple_of(core * HALF, HALF), HALF), :]
    give[...] = total[pl.ds(pl.multiple_of((1 - core) * HALF, HALF), HALF), :]


def sketch_call(place, rows, sketch):
    half = jax.ShapeDtypeStruct((HALF, W), f32)
    return pl.pallas_call(
        sketch_kernel,
        out_shape=(half, half),
        in_specs=[SMEM, HBM, VMEM],
        out_specs=(VMEM, VMEM),
        scratch_shapes=[
            pltpu.VMEM((ROWS, W), bf16),
            pltpu.VMEM((RANK, W), f32),
            pltpu.SemaphoreType.DMA((SKETCH_STEPS,)),
        ],
        compiler_params=params(52),
        name="sketch",
    )(place, rows, sketch)


def sum_core_kernel(keep, got, slots, out):
    out[0:HALF, :] = keep[...] + got[...]
    out[HALF:, :] = jnp.zeros((8, W), f32)
    out[HALF:, 0:128] = slots[...]


def sum_first_kernel(r0, r1, r2, r3, out):
    out[0:HALF, :] = (r0[0:HALF, :] + r2[0:HALF, :]) + (r1[0:HALF, :] + r3[0:HALF, :])
    for k, r in enumerate((r0, r1, r2, r3)):
        out[HALF:, k * 128 : (k + 1) * 128] = r[HALF:, 0:128]


def sum_second_kernel(r0, r1, r2, r3, out):
    out[0:HALF, :] = (r0[0:HALF, :] + r2[0:HALF, :]) + (r1[0:HALF, :] + r3[0:HALF, :])
    for k, r in enumerate((r0, r1, r2, r3)):
        out[HALF + 8 * k : HALF + 8 * (k + 1), :] = r[HALF:, :]


def small_call(kernel, rows, name, *args):
    return pl.pallas_call(
        kernel,
        out_shape=jax.ShapeDtypeStruct((rows, W), f32),
        in_specs=[VMEM] * len(args),
        out_specs=VMEM,
        compiler_params=params(),
        name=name,
    )(*args)


def factor_kernel(place, own, other, rows_hbm, out, rows, sem):
    copy = pltpu.make_async_copy(rows_hbm, rows, sem)
    copy.start()
    first = place[1] % 2 == 0
    mine, theirs = own[0:HALF, :], other[0:HALF, :]
    summed = jnp.concatenate(
        [jnp.where(first, mine, theirs), jnp.where(first, theirs, mine)], axis=0
    )
    padded = jnp.concatenate([summed, jnp.zeros((96, W), f32)], axis=0)
    gram = lax.dot_general(
        summed, padded, NT, precision=lax.Precision.HIGHEST, preferred_element_type=f32
    )
    lane = lax.broadcasted_iota(i32, (RANK, 128), 1)
    line = lax.broadcasted_iota(i32, (RANK, 128), 0)
    work = gram + jnp.where(lane == line + RANK, 1.0, 0.0)
    for k in range(0, RANK, 2):
        first_column = jnp.broadcast_to(work[:, k : k + 1], (RANK, 128))
        second_column = jnp.broadcast_to(work[:, k + 1 : k + 2], (RANK, 128))
        inverse = 1.0 / first_column[k : k + 1, :]
        first_row = work[k : k + 1, :] * inverse
        second_column = second_column - first_column * (second_column[k : k + 1, :] * inverse)
        second_row = work[k + 1 : k + 2, :] - first_column[k + 1 : k + 2, :] * first_row
        second_row = second_row / second_column[k + 1 : k + 2, :]
        work = work - (
            jnp.where(line > k, first_column, 0.0) * first_row
            + jnp.where(line > k + 1, second_column, 0.0) * second_row
        )
    pivots = jnp.sum(jnp.where(lane == line, work, 0.0), axis=1, keepdims=True)
    inverse = work * lax.rsqrt(pivots)
    shifted = jnp.concatenate([jnp.zeros((32, W), f32), summed, jnp.zeros((64, W), f32)], axis=0)
    basis = jnp.dot(
        inverse, shifted, precision=lax.Precision.HIGHEST, preferred_element_type=f32
    ).astype(bf16)
    copy.wait()
    index = lax.broadcasted_iota(i32, (16, BLOCK), 0)
    scales = jnp.zeros((16, BLOCK), f32)
    for b in range(NB_DEV):
        projected = lax.dot_general(
            basis, rows[b * BLOCK : (b + 1) * BLOCK, :], NT, preferred_element_type=f32
        )
        most = jnp.max(jnp.max(jnp.abs(projected), axis=0, keepdims=True), axis=1, keepdims=True)
        scale = (most + 1e-06).astype(bf16).astype(f32)
        factor = (projected / scale).astype(bf16)
        scales = jnp.where(index == b, scale, scales)
        out[b * RANK : (b + 1) * RANK, :] = factor
    out[NB_DEV * RANK :, :] = scales.astype(bf16)


def factor_call(place, own, other, rows):
    return pl.pallas_call(
        factor_kernel,
        out_shape=jax.ShapeDtypeStruct((MSG, BLOCK), bf16),
        in_specs=[SMEM, VMEM, VMEM, HBM],
        out_specs=VMEM,
        scratch_shapes=[pltpu.VMEM((ROWS, W), bf16), pltpu.SemaphoreType.DMA],
        compiler_params=params(52),
        name="factor",
    )(place, own, other, rows)


def touch_call(x, us, *after):
    return pl.pallas_call(
        lambda *refs: None,
        out_shape=jax.ShapeDtypeStruct(x.shape, x.dtype),
        in_specs=[ANY] * (1 + len(after)),
        out_specs=ANY,
        input_output_aliases={0: 0},
        compiler_params=params(),
        cost_estimate=pl.CostEstimate(
            flops=0, bytes_accessed=int(us * 3.0e6), transcendentals=0
        ),
        name="touch",
    )(x, *after)


def join_call(parts, name, *after):
    heights = [part.shape[0] for part in parts]

    def kernel(*refs):
        at = 0
        for ref, height in zip(refs, heights):
            refs[-1][at : at + height, :] = ref[...]
            at += height

    return pl.pallas_call(
        kernel,
        out_shape=jax.ShapeDtypeStruct((sum(heights), BLOCK), bf16),
        in_specs=[VMEM] * len(parts) + [ANY] * len(after),
        out_specs=VMEM,
        compiler_params=params(),
        name=name,
    )(*parts, *after)


def put_call(whole, part, n):
    def kernel(*refs):
        out, sem = refs[-2:]
        copy = pltpu.make_async_copy(
            refs[-3].at[pl.ds(0, 4 * MSG)], out.at[pl.ds(n * 4 * MSG, 4 * MSG)], sem
        )
        copy.start()
        copy.wait()

    first = whole is None
    return pl.pallas_call(
        kernel,
        out_shape=jax.ShapeDtypeStruct((N_CAND * MSG, BLOCK), bf16),
        in_specs=[ANY] * (1 if first else 2),
        out_specs=ANY,
        input_output_aliases={} if first else {0: 0},
        scratch_shapes=[pltpu.SemaphoreType.DMA],
        compiler_params=params(),
        name="put",
    )(*([part] if first else [whole, part]))


def put_all(parts):
    whole = None
    for n, part in parts:
        whole = put_call(whole, part, n)
    return whole


def with_begins(lists, out):
    begins = (lists // NB_DEV) % N_CAND * MSG + lists % NB_DEV * RANK
    out[0:4, :] = lists[0:4, :]
    out[4:6, :] = begins[0:2, :]
    out[6:8, :] = lists[6:8, :]


def plan_kernel(place, own, other, *refs):
    outs, gathered = refs[:N_SET], refs[N_SET]
    me_set, me = place[0], place[1]
    me_z, me_y, me_core = me // 8, (me // 2) % 4, me % 2
    for core, r in enumerate((own, other)):
        for second in range(4):
            for first in range(4):
                s = (core * 4 + second) * 4 + first
                gathered[s * 8 : (s + 1) * 8, :] = r[
                    HALF + 8 * second : HALF + 8 * (second + 1), first * 128 : (first + 1) * 128
                ]
    fields = jnp.concatenate(
        [gathered[pl.ds(n, N_CAND, stride=8), :] for n in range(8)], axis=0
    ).astype(bf16)
    line = lax.broadcasted_iota(i32, (16, 128), 0)
    lane = lax.broadcasted_iota(i32, (16, 128), 1)
    wanted = ((me_set + line) % N_SET) * N_CAND + me
    hot = jnp.where((lane == wanted) & (line < N_SET), 1.0, 0.0).astype(bf16)
    across = lax.dot_general(hot, fields, NT, preferred_element_type=f32)
    down = lax.dot_general(fields, hot, NT, preferred_element_type=f32)
    n = ENTRIES
    sender = lax.broadcasted_iota(i32, (16, n), 1) % N_CAND
    left = across[:, 0:n] + (sender * NB_DEV - ZERO).astype(f32)
    block = across[:, n : 2 * n].astype(i32)
    owner = block // NB_DEV
    z, y, core = owner // 8, (owner // 2) % 4, owner % 2
    z, y = (z - me_z + 4) % 4, (y - me_y + 4) % 4
    at = jnp.where(core == 0, z * 4 + y, y * 4 + z) + ((core + me_core) % 2) * 16
    right = (at * NB_DEV + block % NB_DEV).astype(f32)
    target = jnp.where(across[:, 3 * n :] != 0, across[:, 2 * n : 3 * n], NT_DEV)
    target_down = jnp.where(down[3 * n :, :] != 0, down[2 * n : 3 * n, :], NT_DEV)
    before = lax.broadcasted_iota(i32, (n, n), 1) < lax.broadcasted_iota(i32, (n, n), 0)
    spots = lax.broadcasted_iota(i32, (n, 128), 1).astype(f32)
    spot = lax.broadcasted_iota(i32, (1, 128), 1)
    line = lax.broadcasted_iota(i32, (8, 128), 0)
    lane = lax.broadcasted_iota(i32, (8, 128), 1)
    row = lax.broadcasted_iota(i32, (16, n), 0)
    for gr in range(N_SET):
        t_down, t_across = target_down[:, gr : gr + 1], target[gr : gr + 1, :]
        rank = jnp.sum(
            jnp.where((t_down == t_across) & before, 1.0, 0.0), axis=1, keepdims=True
        )
        count = jnp.sum(jnp.where(t_down == spots, 1.0, 0.0), axis=0, keepdims=True)
        chunks = (count.astype(i32) + (PER_CHUNK - 1)) // PER_CHUNK
        chunks = jnp.where(spot < NT_DEV, chunks, 0).astype(f32)
        start = jnp.sum(jnp.where(spots < t_down, chunks, 0.0), axis=1, keepdims=True)
        end = jnp.sum(jnp.where(lane <= line, chunks, 0.0), axis=1, keepdims=True)
        target_of = jnp.sum(jnp.where(end <= lane.astype(f32), 1.0, 0.0), axis=0, keepdims=True)
        target_of = jnp.minimum(target_of, NT_DEV - 1)
        pieces = jnp.sum(chunks, axis=1, keepdims=True)
        place_of = jnp.where(t_down < NT_DEV, start * PER_CHUNK + rank, 1000.0)
        chosen = jnp.where(place_of == spots, 1.0, 0.0).astype(bf16)
        both = jnp.where(
            row == 0, left[gr : gr + 1, :], jnp.where(row == 1, right[gr : gr + 1, :], 0.0)
        ).astype(bf16)
        lists = jnp.dot(both, chosen, preferred_element_type=f32)[0:8, :]
        lists = jnp.where(line == 0, lists + ZERO, lists)
        lists = jnp.where(line == 2, target_of, jnp.where(line == 3, pieces, lists))
        lists = jnp.where(line == 6, chunks, lists)
        if gr == 2:
            lists = jnp.concatenate([lists, jnp.zeros((8, 128), f32)], axis=0).astype(bf16)
            outs[gr][...] = jnp.concatenate([lists, jnp.zeros((16, 128), bf16)], axis=1)
        else:
            with_begins(lists.astype(i32), outs[gr])


def plan_call(place, own, other, *after):
    shapes = [jax.ShapeDtypeStruct((8, 128), i32)] * N_SET
    shapes[2] = jax.ShapeDtypeStruct((16, BLOCK), bf16)
    return pl.pallas_call(
        lambda *refs: plan_kernel(*refs[:3], *refs[3 + len(after) :]),
        out_shape=shapes,
        in_specs=[SMEM, VMEM, VMEM] + [ANY] * len(after),
        out_specs=[VMEM] * N_SET,
        scratch_shapes=[pltpu.VMEM((N_CAND * 8, 128), f32)],
        compiler_params=params(),
        name="plan",
    )(place, own, other, *after)


def unpack_call(message):
    def kernel(message, out):
        lists = message[4 * MSG :, 0:128].astype(f32)[0:8, :]
        with_begins(lists.astype(i32), out)

    return pl.pallas_call(
        kernel,
        out_shape=jax.ShapeDtypeStruct((8, 128), i32),
        in_specs=[VMEM],
        out_specs=VMEM,
        compiler_params=params(),
        name="unpack",
    )(message)


def spread(factors, scales):
    for p in range(N_CAND):
        rows = factors[p * MSG + NB_DEV * RANK : (p + 1) * MSG, 0:128].astype(f32)
        scales[p * NB_DEV : (p + 1) * NB_DEV, :] = rows[0:NB_DEV, :]
    scales[ZERO : ZERO + 8, :] = jnp.zeros((8, 128), f32)


def block_at(factors, begin):
    return factors[pl.ds(pl.multiple_of(begin, 16), RANK), :]


def expand(pairs, factors, scales, lefts, rights, totals):
    def chunk(q, side):
        for k in range(PER_CHUNK):
            spot = q * PER_CHUNK + k
            left, right = pairs[0, spot], pairs[1, spot]
            weight = scales[pl.ds(left, 1), :] * scales[pl.ds(right, 1), :]
            weight = jnp.broadcast_to(weight, (RANK, 128)).astype(bf16)
            weight = jnp.concatenate([weight, weight], axis=1)
            here = slice(k * RANK, (k + 1) * RANK)
            lefts[side, here, :] = block_at(factors, pairs[4, spot]) * weight
            rights[side, here, :] = block_at(factors, pairs[5, spot])

    def several(n, last):
        for side in range(TURN):
            chunk(TURN * n + side, side)
        terms = [
            lax.dot_general(lefts[side], rights[side], TN, preferred_element_type=f32)
            for side in range(TURN)
        ]
        for side in range(TURN):
            t = pairs[2, TURN * n + side]
            totals[t] = jnp.where(t == last, totals[t], 0.0) + terms[side]
            last = t
        return last

    lax.fori_loop(0, (pairs[3, 0] + (TURN - 1)) // TURN, several, -1)


def total_of(pairs, t, totals):
    return jnp.where(pairs[6, t] > 0, totals[t], 0.0)


WORK = [
    pltpu.VMEM((ZERO + 8, 128), f32),
    pltpu.VMEM((TURN, RANK * PER_CHUNK, BLOCK), bf16),
    pltpu.VMEM((TURN, RANK * PER_CHUNK, BLOCK), bf16),
    pltpu.VMEM((NT_DEV, BLOCK, BLOCK), f32),
]


def send_call(next_list, last_list, factors, *after):
    def kernel(next_list, last_list, factors, *refs):
        to_next, to_last, scales, lefts, rights, totals = refs[len(after) :]
        spread(factors, scales)
        for pairs, out in ((next_list, to_next), (last_list, to_last)):
            expand(pairs, factors, scales, lefts, rights, totals)
            for t in range(NT_DEV):
                out[t] = total_of(pairs, t, totals).astype(bf16)

    out = jax.ShapeDtypeStruct((NT_DEV, BLOCK, BLOCK), bf16)
    return pl.pallas_call(
        kernel,
        out_shape=(out, out),
        in_specs=[SMEM, SMEM, VMEM] + [ANY] * len(after),
        out_specs=(VMEM, VMEM),
        scratch_shapes=WORK,
        compiler_params=params(),
        name="send_pairs",
    )(next_list, last_list, factors, *after)


def keep_call(pairs, base, factors, *after):
    def kernel(pairs, base, factors, *refs):
        out, scales, lefts, rights, totals = refs[len(after) :]
        spread(factors, scales)
        expand(pairs, factors, scales, lefts, rights, totals)
        for t in range(NT_DEV):
            out[t] = base[t] - total_of(pairs, t, totals)

    return pl.pallas_call(
        kernel,
        out_shape=jax.ShapeDtypeStruct((NT_DEV, BLOCK, BLOCK), f32),
        in_specs=[SMEM, VMEM, VMEM] + [ANY] * len(after),
        out_specs=VMEM,
        scratch_shapes=WORK,
        compiler_params=params(),
        name="keep_pairs",
    )(pairs, base, factors, *after)


def final_call(base, one, two):
    def kernel(base, one, two, out, sems):
        copies = []
        for t in range(NT_DEV):
            base[t] = base[t] - (one[t].astype(f32) + two[t].astype(f32))
            copies.append(pltpu.make_async_copy(base.at[t], out.at[t], sems.at[t]))
            copies[t].start()
        for copy in copies:
            copy.wait()

    return pl.pallas_call(
        kernel,
        out_shape=jax.ShapeDtypeStruct((NT_DEV, BLOCK, BLOCK), f32),
        in_specs=[VMEM] * 3,
        out_specs=ANY,
        scratch_shapes=[pltpu.SemaphoreType.DMA((NT_DEV,))],
        compiler_params=params(),
        name="final",
    )(base, one, two)


def per_device(panel_rows, sketch, accumulator, left_block, right_block, target_slot, slot_valid):
    rows = panel_rows[0]
    place = jnp.stack([lax.axis_index("set"), lax.axis_index("cand")]).astype(i32)

    keep, give = sketch_call(place, rows, sketch[0].T)
    got = from_core(give)
    slots = jnp.concatenate(
        [x[0, 0].T for x in (left_block, right_block, target_slot, slot_valid)], axis=0
    ).astype(f32)
    part = small_call(sum_core_kernel, HALF + 8, "sum_core", keep, got, slots)
    part = small_call(
        sum_first_kernel, HALF + 8, "sum_first", part, *[from_cand(part, 0, k) for k in (1, 2, 3)]
    )
    own = small_call(
        sum_second_kernel, HALF + 32, "sum_second", part, *[from_cand(part, 1, k) for k in (1, 2, 3)]
    )
    other = from_core(own)

    mine = factor_call(place, own, other, rows)
    own_list, next_list, far_list, last_list = plan_call(place, own, other, mine)
    line = join_call([mine] + [from_cand(mine, 0, k) for k in (1, 2, 3)], "join_line", next_list)
    far_line = from_set(join_call([line, far_list], "join_far"), 2)
    here = [line] + [from_cand(line, 1, k) for k in (1, 2, 3)]
    there = [from_core(x) for x in here]
    factors = put_all(
        [p for k in range(4) for p in ((k, here[k]), (4 + k, there[k]))]
    )

    to_next, to_last = send_call(next_list, last_list, factors)
    arrived = [touch_call(x, LAST_US) for x in (from_set(to_next, 3), from_set(to_last, 1))]

    far_here = [far_line] + [from_cand(far_line, 1, k) for k in (1, 2, 3)]
    far_there = [from_core(x) for x in far_here]
    far_factors = put_all(
        [p for k in range(4) for p in ((k, far_here[k]), (4 + k, far_there[k]))]
    )
    base = keep_call(own_list, accumulator[0], factors, to_next)
    base = keep_call(unpack_call(far_line), base, far_factors)
    base = final_call(base, *arrived)
    return base[None]


def solution(mesh):
    placed = (
        P("set", "cand", None),
        P("set", None, None),
        P("set", "cand", None, None),
        P("set", "cand", None, None),
        P("set", "cand", None, None),
        P("set", "cand", None, None),
        P("set", "cand", None, None),
    )
    return jax.shard_map(
        per_device,
        mesh=mesh,
        in_specs=placed,
        out_specs=P("set", "cand", None, None),
        check_vma=False,
    )
```

```python
import jax
import jax.numpy as jnp
from jax import lax
from jax.experimental import pallas as pl
from jax.experimental.pallas import tpu as pltpu
from jax.sharding import PartitionSpec as P

W = 512
RANK = 32
BLOCK = 256
NB_DEV = 8
NT_DEV = 8
N_SET = 4
N_CAND = 32
HALF = RANK // 2
ROWS = NB_DEV * BLOCK
MSG = NB_DEV * RANK + 16
SLOTS = 2
SKETCH_STEPS = 4
PER_CHUNK = 8
TURN = 4
ENTRIES = N_CAND * SLOTS
ZERO = NB_DEV * N_CAND
LAST_US = 0
f32, bf16, i32 = jnp.float32, jnp.bfloat16, jnp.int32
VMEM = pl.BlockSpec(memory_space=pltpu.VMEM)
SMEM = pl.BlockSpec(memory_space=pltpu.SMEM)
ANY = pl.BlockSpec(memory_space=pl.ANY)
HBM = pl.BlockSpec(memory_space=pltpu.HBM)
NT = (((1,), (1,)), ((), ()))
TN = (((0,), (0,)), ((), ()))


def params(mib=40):
    return pltpu.CompilerParams(vmem_limit_bytes=mib * 1024 * 1024)


def from_cand(x, leg, k):
    pairs = []
    for me in range(N_CAND):
        z, y, core = me // 8, (me // 2) % 4, me % 2
        if leg == core:
            y = (y + k) % 4
        else:
            z = (z + k) % 4
        pairs.append((z * 8 + y * 2 + core, me))
    return lax.ppermute(x, "cand", pairs)


def from_three(x, leg):
    opposite = from_cand(x, leg, 2)
    return [from_cand(x, leg, 1), opposite, from_cand(x, leg, 3)]


def from_core(x):
    return lax.ppermute(x, "cand", [(me ^ 1, me) for me in range(N_CAND)])


def from_set(x, d, d_core_1=None):
    pairs = []
    for me_set in range(N_SET):
        for me in range(N_CAND):
            ahead = d if d_core_1 is None or me % 2 == 0 else d_core_1
            pairs.append(((me_set + ahead) % N_SET * N_CAND + me, me_set * N_CAND + me))
    return lax.ppermute(x, ("set", "cand"), pairs)


def sketch_kernel(place, rows_hbm, sketch, keep, give, rows, total, sems):
    copies = []
    for n in range(SKETCH_STEPS):
        part = pl.ds(n * (ROWS // SKETCH_STEPS), ROWS // SKETCH_STEPS)
        copies.append(pltpu.make_async_copy(rows_hbm.at[part], rows.at[part], sems.at[n]))
        copies[n].start()
    summed = jnp.zeros((RANK, W), f32)
    for n in range(SKETCH_STEPS):
        copies[n].wait()
        part = rows[n * (ROWS // SKETCH_STEPS) : (n + 1) * (ROWS // SKETCH_STEPS), :]
        sketched = lax.dot_general(sketch[...], part, NT, preferred_element_type=f32)
        summed += jnp.dot(sketched.astype(bf16), part, preferred_element_type=f32)
    total[...] = summed
    core = place[1] % 2
    keep[...] = total[pl.ds(pl.multiple_of(core * HALF, HALF), HALF), :]
    give[...] = total[pl.ds(pl.multiple_of((1 - core) * HALF, HALF), HALF), :]


def sketch_call(place, rows, sketch):
    half = jax.ShapeDtypeStruct((HALF, W), f32)
    return pl.pallas_call(
        sketch_kernel,
        out_shape=(half, half),
        in_specs=[SMEM, HBM, VMEM],
        out_specs=(VMEM, VMEM),
        scratch_shapes=[
            pltpu.VMEM((ROWS, W), bf16),
            pltpu.VMEM((RANK, W), f32),
            pltpu.SemaphoreType.DMA((SKETCH_STEPS,)),
        ],
        compiler_params=params(52),
        name="sketch",
    )(place, rows, sketch)


def sum_core_kernel(keep, got, slots, out):
    out[0:HALF, :] = keep[...] + got[...]
    out[HALF:, :] = jnp.zeros((8, W), f32)
    out[HALF:, 0:128] = slots[...]


def sum_first_kernel(r0, r1, r2, r3, out):
    out[0:HALF, :] = (r0[0:HALF, :] + r2[0:HALF, :]) + (r1[0:HALF, :] + r3[0:HALF, :])
    for k, r in enumerate((r0, r1, r2, r3)):
        out[HALF:, k * 128 : (k + 1) * 128] = r[HALF:, 0:128]


def sum_second_kernel(r0, r1, r2, r3, out):
    out[0:HALF, :] = (r0[0:HALF, :] + r2[0:HALF, :]) + (r1[0:HALF, :] + r3[0:HALF, :])
    for k, r in enumerate((r0, r1, r2, r3)):
        out[HALF + 8 * k : HALF + 8 * (k + 1), :] = r[HALF:, :]


def small_call(kernel, rows, name, *args):
    return pl.pallas_call(
        kernel,
        out_shape=jax.ShapeDtypeStruct((rows, W), f32),
        in_specs=[VMEM] * len(args),
        out_specs=VMEM,
        compiler_params=params(),
        name=name,
    )(*args)


def factor_kernel(place, own, other, rows_hbm, out, rows, sem):
    copy = pltpu.make_async_copy(rows_hbm, rows, sem)
    copy.start()
    first = place[1] % 2 == 0
    mine, theirs = own[0:HALF, :], other[0:HALF, :]
    summed = jnp.concatenate(
        [jnp.where(first, mine, theirs), jnp.where(first, theirs, mine)], axis=0
    )
    padded = jnp.concatenate([summed, jnp.zeros((96, W), f32)], axis=0)
    gram = lax.dot_general(
        summed, padded, NT, precision=lax.Precision.HIGHEST, preferred_element_type=f32
    )
    lane = lax.broadcasted_iota(i32, (RANK, 128), 1)
    line = lax.broadcasted_iota(i32, (RANK, 128), 0)
    work = gram + jnp.where(lane == line + RANK, 1.0, 0.0)
    for k in range(0, RANK, 2):
        first_column = jnp.broadcast_to(work[:, k : k + 1], (RANK, 128))
        second_column = jnp.broadcast_to(work[:, k + 1 : k + 2], (RANK, 128))
        inverse = 1.0 / first_column[k : k + 1, :]
        first_row = work[k : k + 1, :] * inverse
        second_column = second_column - first_column * (second_column[k : k + 1, :] * inverse)
        second_row = work[k + 1 : k + 2, :] - first_column[k + 1 : k + 2, :] * first_row
        second_row = second_row / second_column[k + 1 : k + 2, :]
        work = work - (
            jnp.where(line > k, first_column, 0.0) * first_row
            + jnp.where(line > k + 1, second_column, 0.0) * second_row
        )
    pivots = jnp.sum(jnp.where(lane == line, work, 0.0), axis=1, keepdims=True)
    inverse = work * lax.rsqrt(pivots)
    shifted = jnp.concatenate([jnp.zeros((32, W), f32), summed, jnp.zeros((64, W), f32)], axis=0)
    basis = jnp.dot(
        inverse, shifted, precision=lax.Precision.HIGHEST, preferred_element_type=f32
    ).astype(bf16)
    copy.wait()
    index = lax.broadcasted_iota(i32, (16, BLOCK), 0)
    scales = jnp.zeros((16, BLOCK), f32)
    for b in range(NB_DEV):
        projected = lax.dot_general(
            basis, rows[b * BLOCK : (b + 1) * BLOCK, :], NT, preferred_element_type=f32
        )
        most = jnp.max(jnp.max(jnp.abs(projected), axis=0, keepdims=True), axis=1, keepdims=True)
        scale = (most + 1e-06).astype(bf16).astype(f32)
        factor = (projected / scale).astype(bf16)
        scales = jnp.where(index == b, scale, scales)
        out[b * RANK : (b + 1) * RANK, :] = factor
    out[NB_DEV * RANK :, :] = scales.astype(bf16)


def factor_call(place, own, other, rows):
    return pl.pallas_call(
        factor_kernel,
        out_shape=jax.ShapeDtypeStruct((MSG, BLOCK), bf16),
        in_specs=[SMEM, VMEM, VMEM, HBM],
        out_specs=VMEM,
        scratch_shapes=[pltpu.VMEM((ROWS, W), bf16), pltpu.SemaphoreType.DMA],
        compiler_params=params(52),
        name="factor",
    )(place, own, other, rows)


def touch_call(x, us, *after):
    return pl.pallas_call(
        lambda *refs: None,
        out_shape=jax.ShapeDtypeStruct(x.shape, x.dtype),
        in_specs=[ANY] * (1 + len(after)),
        out_specs=ANY,
        input_output_aliases={0: 0},
        compiler_params=params(),
        cost_estimate=pl.CostEstimate(
            flops=0, bytes_accessed=int(us * 3.0e6), transcendentals=0
        ),
        name="touch",
    )(x, *after)


def join_call(parts, name, *after):
    heights = [part.shape[0] for part in parts]

    def kernel(*refs):
        at = 0
        for ref, height in zip(refs, heights):
            refs[-1][at : at + height, :] = ref[...]
            at += height

    return pl.pallas_call(
        kernel,
        out_shape=jax.ShapeDtypeStruct((sum(heights), BLOCK), bf16),
        in_specs=[VMEM] * len(parts) + [ANY] * len(after),
        out_specs=VMEM,
        compiler_params=params(),
        name=name,
    )(*parts, *after)


def put_call(whole, part, n):
    def kernel(*refs):
        out, sem = refs[-2:]
        copy = pltpu.make_async_copy(
            refs[-3].at[pl.ds(0, 4 * MSG)], out.at[pl.ds(n * 4 * MSG, 4 * MSG)], sem
        )
        copy.start()
        copy.wait()

    first = whole is None
    return pl.pallas_call(
        kernel,
        out_shape=jax.ShapeDtypeStruct((N_CAND * MSG, BLOCK), bf16),
        in_specs=[ANY] * (1 if first else 2),
        out_specs=ANY,
        input_output_aliases={} if first else {0: 0},
        scratch_shapes=[pltpu.SemaphoreType.DMA],
        compiler_params=params(),
        name="put",
    )(*([part] if first else [whole, part]))


def put_all(parts):
    whole = None
    for n, part in parts:
        whole = put_call(whole, part, n)
    return whole


def with_begins(lists, out):
    begins = (lists // NB_DEV) % N_CAND * MSG + lists % NB_DEV * RANK
    out[0:4, :] = lists[0:4, :]
    out[4:6, :] = begins[0:2, :]
    out[6:8, :] = lists[6:8, :]


def plan_kernel(place, own, other, *refs):
    outs, gathered = refs[:N_SET], refs[N_SET]
    me_set, me = place[0], place[1]
    me_z, me_y, me_core = me // 8, (me // 2) % 4, me % 2
    for core, r in enumerate((own, other)):
        for second in range(4):
            for first in range(4):
                s = (core * 4 + second) * 4 + first
                gathered[s * 8 : (s + 1) * 8, :] = r[
                    HALF + 8 * second : HALF + 8 * (second + 1), first * 128 : (first + 1) * 128
                ]
    fields = jnp.concatenate(
        [gathered[pl.ds(n, N_CAND, stride=8), :] for n in range(8)], axis=0
    ).astype(bf16)
    line = lax.broadcasted_iota(i32, (16, 128), 0)
    lane = lax.broadcasted_iota(i32, (16, 128), 1)
    ahead = line + jnp.where(line % 2 == 1, 2 * me_core, 0)
    wanted = ((me_set + ahead) % N_SET) * N_CAND + me
    hot = jnp.where((lane == wanted) & (line < N_SET), 1.0, 0.0).astype(bf16)
    across = lax.dot_general(hot, fields, NT, preferred_element_type=f32)
    down = lax.dot_general(fields, hot, NT, preferred_element_type=f32)
    n = ENTRIES
    sender = lax.broadcasted_iota(i32, (16, n), 1) % N_CAND
    left = across[:, 0:n] + (sender * NB_DEV - ZERO).astype(f32)
    block = across[:, n : 2 * n].astype(i32)
    owner = block // NB_DEV
    z, y, core = owner // 8, (owner // 2) % 4, owner % 2
    z, y = (z - me_z + 4) % 4, (y - me_y + 4) % 4
    at = jnp.where(core == 0, z * 4 + y, y * 4 + z) + ((core + me_core) % 2) * 16
    right = (at * NB_DEV + block % NB_DEV).astype(f32)
    target = jnp.where(across[:, 3 * n :] != 0, across[:, 2 * n : 3 * n], NT_DEV)
    target_down = jnp.where(down[3 * n :, :] != 0, down[2 * n : 3 * n, :], NT_DEV)
    before = lax.broadcasted_iota(i32, (n, n), 1) < lax.broadcasted_iota(i32, (n, n), 0)
    spots = lax.broadcasted_iota(i32, (n, 128), 1).astype(f32)
    spot = lax.broadcasted_iota(i32, (1, 128), 1)
    line = lax.broadcasted_iota(i32, (8, 128), 0)
    lane = lax.broadcasted_iota(i32, (8, 128), 1)
    row = lax.broadcasted_iota(i32, (16, n), 0)
    for gr in range(N_SET):
        t_down, t_across = target_down[:, gr : gr + 1], target[gr : gr + 1, :]
        rank = jnp.sum(
            jnp.where((t_down == t_across) & before, 1.0, 0.0), axis=1, keepdims=True
        )
        count = jnp.sum(jnp.where(t_down == spots, 1.0, 0.0), axis=0, keepdims=True)
        chunks = (count.astype(i32) + (PER_CHUNK - 1)) // PER_CHUNK
        chunks = jnp.where(spot < NT_DEV, chunks, 0).astype(f32)
        start = jnp.sum(jnp.where(spots < t_down, chunks, 0.0), axis=1, keepdims=True)
        end = jnp.sum(jnp.where(lane <= line, chunks, 0.0), axis=1, keepdims=True)
        target_of = jnp.sum(jnp.where(end <= lane.astype(f32), 1.0, 0.0), axis=0, keepdims=True)
        target_of = jnp.minimum(target_of, NT_DEV - 1)
        pieces = jnp.sum(chunks, axis=1, keepdims=True)
        place_of = jnp.where(t_down < NT_DEV, start * PER_CHUNK + rank, 1000.0)
        chosen = jnp.where(place_of == spots, 1.0, 0.0).astype(bf16)
        both = jnp.where(
            row == 0, left[gr : gr + 1, :], jnp.where(row == 1, right[gr : gr + 1, :], 0.0)
        ).astype(bf16)
        lists = jnp.dot(both, chosen, preferred_element_type=f32)[0:8, :]
        lists = jnp.where(line == 0, lists + ZERO, lists)
        lists = jnp.where(line == 2, target_of, jnp.where(line == 3, pieces, lists))
        lists = jnp.where(line == 6, chunks, lists)
        if gr == 2:
            lists = jnp.concatenate([lists, jnp.zeros((8, 128), f32)], axis=0).astype(bf16)
            outs[gr][...] = jnp.concatenate([lists, jnp.zeros((16, 128), bf16)], axis=1)
        else:
            with_begins(lists.astype(i32), outs[gr])


def plan_call(place, own, other, *after):
    shapes = [jax.ShapeDtypeStruct((8, 128), i32)] * N_SET
    shapes[2] = jax.ShapeDtypeStruct((16, BLOCK), bf16)
    return pl.pallas_call(
        lambda *refs: plan_kernel(*refs[:3], *refs[3 + len(after) :]),
        out_shape=shapes,
        in_specs=[SMEM, VMEM, VMEM] + [ANY] * len(after),
        out_specs=[VMEM] * N_SET,
        scratch_shapes=[pltpu.VMEM((N_CAND * 8, 128), f32)],
        compiler_params=params(),
        name="plan",
    )(place, own, other, *after)


def unpack_call(message):
    def kernel(message, out):
        lists = message[4 * MSG :, 0:128].astype(f32)[0:8, :]
        with_begins(lists.astype(i32), out)

    return pl.pallas_call(
        kernel,
        out_shape=jax.ShapeDtypeStruct((8, 128), i32),
        in_specs=[VMEM],
        out_specs=VMEM,
        compiler_params=params(),
        name="unpack",
    )(message)


def spread(factors, scales):
    for p in range(N_CAND):
        rows = factors[p * MSG + NB_DEV * RANK : (p + 1) * MSG, 0:128].astype(f32)
        scales[p * NB_DEV : (p + 1) * NB_DEV, :] = rows[0:NB_DEV, :]
    scales[ZERO : ZERO + 8, :] = jnp.zeros((8, 128), f32)


def block_at(factors, begin):
    return factors[pl.ds(pl.multiple_of(begin, 16), RANK), :]


def expand(pairs, factors, scales, lefts, rights, totals):
    def chunk(q, side):
        for k in range(PER_CHUNK):
            spot = q * PER_CHUNK + k
            left, right = pairs[0, spot], pairs[1, spot]
            weight = scales[pl.ds(left, 1), :] * scales[pl.ds(right, 1), :]
            weight = jnp.broadcast_to(weight, (RANK, 128)).astype(bf16)
            weight = jnp.concatenate([weight, weight], axis=1)
            here = slice(k * RANK, (k + 1) * RANK)
            lefts[side, here, :] = block_at(factors, pairs[4, spot]) * weight
            rights[side, here, :] = block_at(factors, pairs[5, spot])

    def several(n, last):
        for side in range(TURN):
            chunk(TURN * n + side, side)
        terms = [
            lax.dot_general(lefts[side], rights[side], TN, preferred_element_type=f32)
            for side in range(TURN)
        ]
        for side in range(TURN):
            t = pairs[2, TURN * n + side]
            totals[t] = jnp.where(t == last, totals[t], 0.0) + terms[side]
            last = t
        return last

    lax.fori_loop(0, (pairs[3, 0] + (TURN - 1)) // TURN, several, -1)


def total_of(pairs, t, totals):
    return jnp.where(pairs[6, t] > 0, totals[t], 0.0)


WORK = [
    pltpu.VMEM((ZERO + 8, 128), f32),
    pltpu.VMEM((TURN, RANK * PER_CHUNK, BLOCK), bf16),
    pltpu.VMEM((TURN, RANK * PER_CHUNK, BLOCK), bf16),
    pltpu.VMEM((NT_DEV, BLOCK, BLOCK), f32),
]


def send_call(one_list, two_list, factors, *after):
    def kernel(one_list, two_list, factors, *refs):
        to_one, to_two, scales, lefts, rights, totals = refs[len(after) :]
        spread(factors, scales)
        for pairs, out in ((one_list, to_one), (two_list, to_two)):
            expand(pairs, factors, scales, lefts, rights, totals)
            for t in range(NT_DEV):
                out[t] = total_of(pairs, t, totals).astype(bf16)

    out = jax.ShapeDtypeStruct((NT_DEV, BLOCK, BLOCK), bf16)
    return pl.pallas_call(
        kernel,
        out_shape=(out, out),
        in_specs=[SMEM, SMEM, VMEM] + [ANY] * len(after),
        out_specs=(VMEM, VMEM),
        scratch_shapes=WORK,
        compiler_params=params(),
        name="send_pairs",
    )(one_list, two_list, factors, *after)


def keep_call(pairs, base, factors, *after):
    def kernel(pairs, base, factors, *refs):
        out, scales, lefts, rights, totals = refs[len(after) :]
        spread(factors, scales)
        expand(pairs, factors, scales, lefts, rights, totals)
        for t in range(NT_DEV):
            out[t] = base[t] - total_of(pairs, t, totals)

    return pl.pallas_call(
        kernel,
        out_shape=jax.ShapeDtypeStruct((NT_DEV, BLOCK, BLOCK), f32),
        in_specs=[SMEM, VMEM, VMEM] + [ANY] * len(after),
        out_specs=VMEM,
        scratch_shapes=WORK,
        compiler_params=params(),
        name="keep_pairs",
    )(pairs, base, factors, *after)


def final_call(base, one, two):
    def kernel(base, one, two, out, sems):
        copies = []
        for t in range(NT_DEV):
            base[t] = base[t] - (one[t].astype(f32) + two[t].astype(f32))
            copies.append(pltpu.make_async_copy(base.at[t], out.at[t], sems.at[t]))
            copies[t].start()
        for copy in copies:
            copy.wait()

    return pl.pallas_call(
        kernel,
        out_shape=jax.ShapeDtypeStruct((NT_DEV, BLOCK, BLOCK), f32),
        in_specs=[VMEM] * 3,
        out_specs=ANY,
        scratch_shapes=[pltpu.SemaphoreType.DMA((NT_DEV,))],
        compiler_params=params(),
        name="final",
    )(base, one, two)


def per_device(panel_rows, sketch, accumulator, left_block, right_block, target_slot, slot_valid):
    rows = panel_rows[0]
    place = jnp.stack([lax.axis_index("set"), lax.axis_index("cand")]).astype(i32)

    keep, give = sketch_call(place, rows, sketch[0].T)
    got = from_core(give)
    slots = jnp.concatenate(
        [x[0, 0].T for x in (left_block, right_block, target_slot, slot_valid)], axis=0
    ).astype(f32)
    part = small_call(sum_core_kernel, HALF + 8, "sum_core", keep, got, slots)
    part = small_call(
        sum_first_kernel, HALF + 8, "sum_first", part, *from_three(part, 0)
    )
    own = small_call(
        sum_second_kernel, HALF + 32, "sum_second", part, *from_three(part, 1)
    )
    other = from_core(own)

    mine = factor_call(place, own, other, rows)
    own_list, one_list, far_list, two_list = plan_call(place, own, other, mine)
    line = join_call([mine] + from_three(mine, 0), "join_line", one_list)
    far_line = from_set(join_call([line, far_list], "join_far"), 2)
    here = [line] + from_three(line, 1)
    factors = put_all([(k, here[k]) for k in range(3)])
    here[3] = touch_call(here[3], 0, factors)
    factors = put_call(factors, here[3], 3)
    for k in range(4):
        factors = put_call(factors, from_core(here[k]), 4 + k)

    to_one, to_two = send_call(one_list, two_list, factors)
    arrived = [touch_call(x, LAST_US) for x in (from_set(to_one, 3, 1), from_set(to_two, 1, 3))]

    far_here = [far_line] + from_three(far_line, 1)
    far_there = [from_core(x) for x in far_here]
    far_factors = put_all(
        [p for k in range(4) for p in ((k, far_here[k]), (4 + k, far_there[k]))]
    )
    base = keep_call(own_list, accumulator[0], factors, to_one)
    base = keep_call(unpack_call(far_line), base, far_factors)
    base = final_call(base, *arrived)
    return base[None]


def solution(mesh):
    placed = (
        P("set", "cand", None),
        P("set", None, None),
        P("set", "cand", None, None),
        P("set", "cand", None, None),
        P("set", "cand", None, None),
        P("set", "cand", None, None),
        P("set", "cand", None, None),
    )
    return jax.shard_map(
        per_device,
        mesh=mesh,
        in_specs=placed,
        out_specs=P("set", "cand", None, None),
        check_vma=False,
    )
```

```python
import jax
import jax.numpy as jnp
from jax import lax
from jax.experimental import pallas as pl
from jax.experimental.pallas import tpu as pltpu
from jax.sharding import PartitionSpec as P

W = 512
RANK = 32
BLOCK = 256
NB_DEV = 8
NT_DEV = 8
N_SET = 4
N_CAND = 32
HALF = RANK // 2
ROWS = NB_DEV * BLOCK
MSG = NB_DEV * RANK + 16
SLOTS = 2
SKETCH_STEPS = 4
PER_CHUNK = 8
TURN = 4
ENTRIES = N_CAND * SLOTS
ZERO = NB_DEV * N_CAND
LAST_US = 0
f32, bf16, i32 = jnp.float32, jnp.bfloat16, jnp.int32
VMEM = pl.BlockSpec(memory_space=pltpu.VMEM)
SMEM = pl.BlockSpec(memory_space=pltpu.SMEM)
ANY = pl.BlockSpec(memory_space=pl.ANY)
HBM = pl.BlockSpec(memory_space=pltpu.HBM)
NT = (((1,), (1,)), ((), ()))
TN = (((0,), (0,)), ((), ()))


def params(mib=40):
    return pltpu.CompilerParams(vmem_limit_bytes=mib * 1024 * 1024)


def from_cand(x, leg, k):
    pairs = []
    for me in range(N_CAND):
        z, y, core = me // 8, (me // 2) % 4, me % 2
        if leg == core:
            y = (y + k) % 4
        else:
            z = (z + k) % 4
        pairs.append((z * 8 + y * 2 + core, me))
    return lax.ppermute(x, "cand", pairs)


def from_core(x):
    return lax.ppermute(x, "cand", [(me ^ 1, me) for me in range(N_CAND)])


def from_set(x, d):
    return lax.ppermute(x, "set", [((me + d) % N_SET, me) for me in range(N_SET)])


def sketch_kernel(place, rows_hbm, sketch, keep, give, rows, total, sems):
    copies = []
    for n in range(SKETCH_STEPS):
        part = pl.ds(n * (ROWS // SKETCH_STEPS), ROWS // SKETCH_STEPS)
        copies.append(pltpu.make_async_copy(rows_hbm.at[part], rows.at[part], sems.at[n]))
        copies[n].start()
    summed = jnp.zeros((RANK, W), f32)
    for n in range(SKETCH_STEPS):
        copies[n].wait()
        part = rows[n * (ROWS // SKETCH_STEPS) : (n + 1) * (ROWS // SKETCH_STEPS), :]
        sketched = lax.dot_general(sketch[...], part, NT, preferred_element_type=f32)
        summed += jnp.dot(sketched.astype(bf16), part, preferred_element_type=f32)
    total[...] = summed
    core = place[1] % 2
    keep[...] = total[pl.ds(pl.multiple_of(core * HALF, HALF), HALF), :]
    give[...] = total[pl.ds(pl.multiple_of((1 - core) * HALF, HALF), HALF), :]


def sketch_call(place, rows, sketch):
    half = jax.ShapeDtypeStruct((HALF, W), f32)
    return pl.pallas_call(
        sketch_kernel,
        out_shape=(half, half),
        in_specs=[SMEM, HBM, VMEM],
        out_specs=(VMEM, VMEM),
        scratch_shapes=[
            pltpu.VMEM((ROWS, W), bf16),
            pltpu.VMEM((RANK, W), f32),
            pltpu.SemaphoreType.DMA((SKETCH_STEPS,)),
        ],
        compiler_params=params(52),
        name="sketch",
    )(place, rows, sketch)


def sum_core_kernel(keep, got, slots, out):
    out[0:HALF, :] = keep[...] + got[...]
    out[HALF:, :] = jnp.zeros((8, W), f32)
    out[HALF:, 0:128] = slots[...]


def sum_first_kernel(r0, r1, r2, r3, out):
    out[0:HALF, :] = (r0[0:HALF, :] + r2[0:HALF, :]) + (r1[0:HALF, :] + r3[0:HALF, :])
    for k, r in enumerate((r0, r1, r2, r3)):
        out[HALF:, k * 128 : (k + 1) * 128] = r[HALF:, 0:128]


def sum_second_kernel(r0, r1, r2, r3, out):
    out[0:HALF, :] = (r0[0:HALF, :] + r2[0:HALF, :]) + (r1[0:HALF, :] + r3[0:HALF, :])
    for k, r in enumerate((r0, r1, r2, r3)):
        out[HALF + 8 * k : HALF + 8 * (k + 1), :] = r[HALF:, :]


def small_call(kernel, rows, name, *args):
    return pl.pallas_call(
        kernel,
        out_shape=jax.ShapeDtypeStruct((rows, W), f32),
        in_specs=[VMEM] * len(args),
        out_specs=VMEM,
        compiler_params=params(),
        name=name,
    )(*args)


def factor_kernel(place, own, other, rows_hbm, out, rows, sem):
    copy = pltpu.make_async_copy(rows_hbm, rows, sem)
    copy.start()
    first = place[1] % 2 == 0
    mine, theirs = own[0:HALF, :], other[0:HALF, :]
    summed = jnp.concatenate(
        [jnp.where(first, mine, theirs), jnp.where(first, theirs, mine)], axis=0
    )
    padded = jnp.concatenate([summed, jnp.zeros((96, W), f32)], axis=0)
    gram = lax.dot_general(
        summed, padded, NT, precision=lax.Precision.HIGHEST, preferred_element_type=f32
    )
    lane = lax.broadcasted_iota(i32, (RANK, 128), 1)
    line = lax.broadcasted_iota(i32, (RANK, 128), 0)
    work = gram + jnp.where(lane == line + RANK, 1.0, 0.0)
    for k in range(0, RANK, 2):
        first_column = jnp.broadcast_to(work[:, k : k + 1], (RANK, 128))
        second_column = jnp.broadcast_to(work[:, k + 1 : k + 2], (RANK, 128))
        inverse = 1.0 / first_column[k : k + 1, :]
        first_row = work[k : k + 1, :] * inverse
        second_column = second_column - first_column * (second_column[k : k + 1, :] * inverse)
        second_row = work[k + 1 : k + 2, :] - first_column[k + 1 : k + 2, :] * first_row
        second_row = second_row / second_column[k + 1 : k + 2, :]
        work = work - (
            jnp.where(line > k, first_column, 0.0) * first_row
            + jnp.where(line > k + 1, second_column, 0.0) * second_row
        )
    pivots = jnp.sum(jnp.where(lane == line, work, 0.0), axis=1, keepdims=True)
    inverse = work * lax.rsqrt(pivots)
    shifted = jnp.concatenate([jnp.zeros((32, W), f32), summed, jnp.zeros((64, W), f32)], axis=0)
    basis = jnp.dot(
        inverse, shifted, precision=lax.Precision.HIGHEST, preferred_element_type=f32
    ).astype(bf16)
    copy.wait()
    index = lax.broadcasted_iota(i32, (16, BLOCK), 0)
    scales = jnp.zeros((16, BLOCK), f32)
    for b in range(NB_DEV):
        projected = lax.dot_general(
            basis, rows[b * BLOCK : (b + 1) * BLOCK, :], NT, preferred_element_type=f32
        )
        most = jnp.max(jnp.max(jnp.abs(projected), axis=0, keepdims=True), axis=1, keepdims=True)
        scale = (most + 1e-06).astype(bf16).astype(f32)
        factor = (projected / scale).astype(bf16)
        scales = jnp.where(index == b, scale, scales)
        out[b * RANK : (b + 1) * RANK, :] = factor
    out[NB_DEV * RANK :, :] = scales.astype(bf16)


def factor_call(place, own, other, rows):
    return pl.pallas_call(
        factor_kernel,
        out_shape=jax.ShapeDtypeStruct((MSG, BLOCK), bf16),
        in_specs=[SMEM, VMEM, VMEM, HBM],
        out_specs=VMEM,
        scratch_shapes=[pltpu.VMEM((ROWS, W), bf16), pltpu.SemaphoreType.DMA],
        compiler_params=params(52),
        name="factor",
    )(place, own, other, rows)


def touch_call(x, us, *after):
    return pl.pallas_call(
        lambda *refs: None,
        out_shape=jax.ShapeDtypeStruct(x.shape, x.dtype),
        in_specs=[ANY] * (1 + len(after)),
        out_specs=ANY,
        input_output_aliases={0: 0},
        compiler_params=params(),
        cost_estimate=pl.CostEstimate(
            flops=0, bytes_accessed=int(us * 3.0e6), transcendentals=0
        ),
        name="touch",
    )(x, *after)


def join_call(parts, name, *after):
    heights = [part.shape[0] for part in parts]

    def kernel(*refs):
        at = 0
        for ref, height in zip(refs, heights):
            refs[-1][at : at + height, :] = ref[...]
            at += height

    return pl.pallas_call(
        kernel,
        out_shape=jax.ShapeDtypeStruct((sum(heights), BLOCK), bf16),
        in_specs=[VMEM] * len(parts) + [ANY] * len(after),
        out_specs=VMEM,
        compiler_params=params(),
        name=name,
    )(*parts, *after)


def put_call(whole, part, n):
    def kernel(*refs):
        out, sem = refs[-2:]
        copy = pltpu.make_async_copy(
            refs[-3].at[pl.ds(0, 4 * MSG)], out.at[pl.ds(n * 4 * MSG, 4 * MSG)], sem
        )
        copy.start()
        copy.wait()

    first = whole is None
    return pl.pallas_call(
        kernel,
        out_shape=jax.ShapeDtypeStruct((N_CAND * MSG, BLOCK), bf16),
        in_specs=[ANY] * (1 if first else 2),
        out_specs=ANY,
        input_output_aliases={} if first else {0: 0},
        scratch_shapes=[pltpu.SemaphoreType.DMA],
        compiler_params=params(),
        name="put",
    )(*([part] if first else [whole, part]))


def put_all(parts):
    whole = None
    for n, part in parts:
        whole = put_call(whole, part, n)
    return whole


def with_begins(lists, out):
    begins = (lists // NB_DEV) % N_CAND * MSG + lists % NB_DEV * RANK
    out[0:4, :] = lists[0:4, :]
    out[4:6, :] = begins[0:2, :]
    out[6:8, :] = lists[6:8, :]


def plan_kernel(place, own, other, *refs):
    outs, gathered = refs[:N_SET], refs[N_SET]
    me_set, me = place[0], place[1]
    me_z, me_y, me_core = me // 8, (me // 2) % 4, me % 2
    for core, r in enumerate((own, other)):
        for second in range(4):
            for first in range(4):
                s = (core * 4 + second) * 4 + first
                gathered[s * 8 : (s + 1) * 8, :] = r[
                    HALF + 8 * second : HALF + 8 * (second + 1), first * 128 : (first + 1) * 128
                ]
    fields = jnp.concatenate(
        [gathered[pl.ds(n, N_CAND, stride=8), :] for n in range(8)], axis=0
    ).astype(bf16)
    line = lax.broadcasted_iota(i32, (16, 128), 0)
    lane = lax.broadcasted_iota(i32, (16, 128), 1)
    wanted = ((me_set + line) % N_SET) * N_CAND + me
    hot = jnp.where((lane == wanted) & (line < N_SET), 1.0, 0.0).astype(bf16)
    across = lax.dot_general(hot, fields, NT, preferred_element_type=f32)
    down = lax.dot_general(fields, hot, NT, preferred_element_type=f32)
    n = ENTRIES
    sender = lax.broadcasted_iota(i32, (16, n), 1) % N_CAND
    left = across[:, 0:n] + (sender * NB_DEV - ZERO).astype(f32)
    block = across[:, n : 2 * n].astype(i32)
    owner = block // NB_DEV
    z, y, core = owner // 8, (owner // 2) % 4, owner % 2
    z, y = (z - me_z + 4) % 4, (y - me_y + 4) % 4
    at = jnp.where(core == 0, z * 4 + y, y * 4 + z) + ((core + me_core) % 2) * 16
    right = (at * NB_DEV + block % NB_DEV).astype(f32)
    target = jnp.where(across[:, 3 * n :] != 0, across[:, 2 * n : 3 * n], NT_DEV)
    target_down = jnp.where(down[3 * n :, :] != 0, down[2 * n : 3 * n, :], NT_DEV)
    before = lax.broadcasted_iota(i32, (n, n), 1) < lax.broadcasted_iota(i32, (n, n), 0)
    spots = lax.broadcasted_iota(i32, (n, 128), 1).astype(f32)
    spot = lax.broadcasted_iota(i32, (1, 128), 1)
    line = lax.broadcasted_iota(i32, (8, 128), 0)
    lane = lax.broadcasted_iota(i32, (8, 128), 1)
    row = lax.broadcasted_iota(i32, (16, n), 0)
    for gr in range(N_SET):
        t_down, t_across = target_down[:, gr : gr + 1], target[gr : gr + 1, :]
        rank = jnp.sum(
            jnp.where((t_down == t_across) & before, 1.0, 0.0), axis=1, keepdims=True
        )
        count = jnp.sum(jnp.where(t_down == spots, 1.0, 0.0), axis=0, keepdims=True)
        chunks = (count.astype(i32) + (PER_CHUNK - 1)) // PER_CHUNK
        chunks = jnp.where(spot < NT_DEV, chunks, 0).astype(f32)
        start = jnp.sum(jnp.where(spots < t_down, chunks, 0.0), axis=1, keepdims=True)
        end = jnp.sum(jnp.where(lane <= line, chunks, 0.0), axis=1, keepdims=True)
        target_of = jnp.sum(jnp.where(end <= lane.astype(f32), 1.0, 0.0), axis=0, keepdims=True)
        target_of = jnp.minimum(target_of, NT_DEV - 1)
        pieces = jnp.sum(chunks, axis=1, keepdims=True)
        place_of = jnp.where(t_down < NT_DEV, start * PER_CHUNK + rank, 1000.0)
        chosen = jnp.where(place_of == spots, 1.0, 0.0).astype(bf16)
        both = jnp.where(
            row == 0, left[gr : gr + 1, :], jnp.where(row == 1, right[gr : gr + 1, :], 0.0)
        ).astype(bf16)
        lists = jnp.dot(both, chosen, preferred_element_type=f32)[0:8, :]
        lists = jnp.where(line == 0, lists + ZERO, lists)
        lists = jnp.where(line == 2, target_of, jnp.where(line == 3, pieces, lists))
        lists = jnp.where(line == 6, chunks, lists)
        if gr == 2:
            lists = jnp.concatenate([lists, jnp.zeros((8, 128), f32)], axis=0).astype(bf16)
            outs[gr][...] = jnp.concatenate([lists, jnp.zeros((16, 128), bf16)], axis=1)
        else:
            with_begins(lists.astype(i32), outs[gr])


def plan_call(place, own, other, *after):
    shapes = [jax.ShapeDtypeStruct((8, 128), i32)] * N_SET
    shapes[2] = jax.ShapeDtypeStruct((16, BLOCK), bf16)
    return pl.pallas_call(
        lambda *refs: plan_kernel(*refs[:3], *refs[3 + len(after) :]),
        out_shape=shapes,
        in_specs=[SMEM, VMEM, VMEM] + [ANY] * len(after),
        out_specs=[VMEM] * N_SET,
        scratch_shapes=[pltpu.VMEM((N_CAND * 8, 128), f32)],
        compiler_params=params(),
        name="plan",
    )(place, own, other, *after)


def unpack_call(message):
    def kernel(message, out):
        lists = message[4 * MSG :, 0:128].astype(f32)[0:8, :]
        with_begins(lists.astype(i32), out)

    return pl.pallas_call(
        kernel,
        out_shape=jax.ShapeDtypeStruct((8, 128), i32),
        in_specs=[VMEM],
        out_specs=VMEM,
        compiler_params=params(),
        name="unpack",
    )(message)


def spread(factors, scales):
    for p in range(N_CAND):
        rows = factors[p * MSG + NB_DEV * RANK : (p + 1) * MSG, 0:128].astype(f32)
        scales[p * NB_DEV : (p + 1) * NB_DEV, :] = rows[0:NB_DEV, :]
    scales[ZERO : ZERO + 8, :] = jnp.zeros((8, 128), f32)


def block_at(factors, begin):
    return factors[pl.ds(pl.multiple_of(begin, 16), RANK), :]


def expand(pairs, factors, scales, lefts, rights, totals):
    def chunk(q, side):
        for k in range(PER_CHUNK):
            spot = q * PER_CHUNK + k
            left, right = pairs[0, spot], pairs[1, spot]
            weight = scales[pl.ds(left, 1), :] * scales[pl.ds(right, 1), :]
            weight = jnp.broadcast_to(weight, (RANK, 128)).astype(bf16)
            weight = jnp.concatenate([weight, weight], axis=1)
            here = slice(k * RANK, (k + 1) * RANK)
            lefts[side, here, :] = block_at(factors, pairs[4, spot]) * weight
            rights[side, here, :] = block_at(factors, pairs[5, spot])

    def several(n, last):
        for side in range(TURN):
            chunk(TURN * n + side, side)
        terms = [
            lax.dot_general(lefts[side], rights[side], TN, preferred_element_type=f32)
            for side in range(TURN)
        ]
        for side in range(TURN):
            t = pairs[2, TURN * n + side]
            totals[t] = jnp.where(t == last, totals[t], 0.0) + terms[side]
            last = t
        return last

    lax.fori_loop(0, (pairs[3, 0] + (TURN - 1)) // TURN, several, -1)


def total_of(pairs, t, totals):
    return jnp.where(pairs[6, t] > 0, totals[t], 0.0)


WORK = [
    pltpu.VMEM((ZERO + 8, 128), f32),
    pltpu.VMEM((TURN, RANK * PER_CHUNK, BLOCK), bf16),
    pltpu.VMEM((TURN, RANK * PER_CHUNK, BLOCK), bf16),
    pltpu.VMEM((NT_DEV, BLOCK, BLOCK), f32),
]


def expand2(lists, factors, scales, lefts, rights, totals):
    def chunk(pairs, q, side):
        for k in range(PER_CHUNK):
            spot = q * PER_CHUNK + k
            left, right = pairs[0, spot], pairs[1, spot]
            weight = scales[pl.ds(left, 1), :] * scales[pl.ds(right, 1), :]
            weight = jnp.broadcast_to(weight, (RANK, 128)).astype(bf16)
            weight = jnp.concatenate([weight, weight], axis=1)
            here = slice(k * RANK, (k + 1) * RANK)
            lefts[side, here, :] = block_at(factors, pairs[4, spot]) * weight
            rights[side, here, :] = block_at(factors, pairs[5, spot])

    def couple(n, last):
        for l in range(2):
            for i in range(4):
                chunk(lists[l], 4 * n + i, l * 4 + i)
        terms = [
            lax.dot_general(lefts[side], rights[side], TN, preferred_element_type=f32)
            for side in range(8)
        ]
        last = list(last)
        for l in range(2):
            for i in range(4):
                t = lists[l][2, 4 * n + i]
                totals[l, t] = jnp.where(t == last[l], totals[l, t], 0.0) + terms[l * 4 + i]
                last[l] = t
        return tuple(last)

    most = jnp.maximum(lists[0][3, 0], lists[1][3, 0])
    lax.fori_loop(0, (most + 3) // 4, couple, (-1, -1))


def send_call(next_list, last_list, factors):
    def kernel(next_list, last_list, factors, to_next, to_last, scales, lefts, rights, totals):
        spread(factors, scales)
        expand2((next_list, last_list), factors, scales, lefts, rights, totals)
        for l, (pairs, out) in enumerate(((next_list, to_next), (last_list, to_last))):
            for t in range(NT_DEV):
                out[t] = total_of(pairs, t, totals.at[l]).astype(bf16)

    out = jax.ShapeDtypeStruct((NT_DEV, BLOCK, BLOCK), bf16)
    work = [
        pltpu.VMEM((ZERO + 8, 128), f32),
        pltpu.VMEM((8, RANK * PER_CHUNK, BLOCK), bf16),
        pltpu.VMEM((8, RANK * PER_CHUNK, BLOCK), bf16),
        pltpu.VMEM((2, NT_DEV, BLOCK, BLOCK), f32),
    ]
    return pl.pallas_call(
        kernel,
        out_shape=(out, out),
        in_specs=[SMEM, SMEM, VMEM],
        out_specs=(VMEM, VMEM),
        scratch_shapes=work,
        compiler_params=params(),
        name="send_pairs",
    )(next_list, last_list, factors)


def keep_call(pairs, base, factors, *after):
    def kernel(pairs, base, factors, *refs):
        out, scales, lefts, rights, totals = refs[len(after) :]
        spread(factors, scales)
        expand(pairs, factors, scales, lefts, rights, totals)
        for t in range(NT_DEV):
            out[t] = base[t] - total_of(pairs, t, totals)

    return pl.pallas_call(
        kernel,
        out_shape=jax.ShapeDtypeStruct((NT_DEV, BLOCK, BLOCK), f32),
        in_specs=[SMEM, VMEM, VMEM] + [ANY] * len(after),
        out_specs=VMEM,
        scratch_shapes=WORK,
        compiler_params=params(),
        name="keep_pairs",
    )(pairs, base, factors, *after)


def final_call(base, one, two):
    def kernel(base, one, two, out, sems):
        copies = []
        for t in range(NT_DEV):
            base[t] = base[t] - (one[t].astype(f32) + two[t].astype(f32))
            copies.append(pltpu.make_async_copy(base.at[t], out.at[t], sems.at[t]))
            copies[t].start()
        for copy in copies:
            copy.wait()

    return pl.pallas_call(
        kernel,
        out_shape=jax.ShapeDtypeStruct((NT_DEV, BLOCK, BLOCK), f32),
        in_specs=[VMEM] * 3,
        out_specs=ANY,
        scratch_shapes=[pltpu.SemaphoreType.DMA((NT_DEV,))],
        compiler_params=params(),
        name="final",
    )(base, one, two)


def per_device(panel_rows, sketch, accumulator, left_block, right_block, target_slot, slot_valid):
    rows = panel_rows[0]
    place = jnp.stack([lax.axis_index("set"), lax.axis_index("cand")]).astype(i32)

    keep, give = sketch_call(place, rows, sketch[0].T)
    got = from_core(give)
    slots = jnp.concatenate(
        [x[0, 0].T for x in (left_block, right_block, target_slot, slot_valid)], axis=0
    ).astype(f32)
    part = small_call(sum_core_kernel, HALF + 8, "sum_core", keep, got, slots)
    part = small_call(
        sum_first_kernel, HALF + 8, "sum_first", part, *[from_cand(part, 0, k) for k in (1, 2, 3)]
    )
    own = small_call(
        sum_second_kernel, HALF + 32, "sum_second", part, *[from_cand(part, 1, k) for k in (1, 2, 3)]
    )
    other = from_core(own)

    mine = factor_call(place, own, other, rows)
    own_list, next_list, far_list, last_list = plan_call(place, own, other, mine)
    line = join_call([mine] + [from_cand(mine, 0, k) for k in (1, 2, 3)], "join_line", next_list)
    far_line = from_set(join_call([line, far_list], "join_far"), 2)
    here = [line] + [from_cand(line, 1, k) for k in (1, 2, 3)]
    there = [from_core(x) for x in here]
    factors = put_all(
        [p for k in range(4) for p in ((k, here[k]), (4 + k, there[k]))]
    )

    to_next, to_last = send_call(next_list, last_list, factors)
    arrived = [touch_call(x, LAST_US) for x in (from_set(to_next, 3), from_set(to_last, 1))]

    far_here = [far_line] + [from_cand(far_line, 1, k) for k in (1, 2, 3)]
    far_there = [from_core(x) for x in far_here]
    far_factors = put_all(
        [p for k in range(4) for p in ((k, far_here[k]), (4 + k, far_there[k]))]
    )
    base = keep_call(own_list, accumulator[0], factors, to_next)
    base = keep_call(unpack_call(far_line), base, far_factors)
    base = final_call(base, *arrived)
    return base[None]


def solution(mesh):
    placed = (
        P("set", "cand", None),
        P("set", None, None),
        P("set", "cand", None, None),
        P("set", "cand", None, None),
        P("set", "cand", None, None),
        P("set", "cand", None, None),
        P("set", "cand", None, None),
    )
    return jax.shard_map(
        per_device,
        mesh=mesh,
        in_specs=placed,
        out_specs=P("set", "cand", None, None),
        check_vma=False,
    )
```
